512 devices in a mesh: ad: 64 (over x, y, core), tp: 8 (over z).
Axes of the slice: x: 4, y: 8, z: 8, core: 2. Of those that a mesh axis runs over, the one named last changes fastest.
Arguments:
- inputs: bfloat16 [512, 8192], P('ad', 'tp'), may hold values from -6 to 6
- w_gate: bfloat16 [28672, 8192], P('ad', 'tp'), may hold values from -0.0625 to 0.0625
- w_up: bfloat16 [28672, 8192], P('ad', 'tp'), may hold values from -0.0625 to 0.0625
- w_down: bfloat16 [28672, 8192], P('ad', 'tp'), may hold values from -0.03125 to 0.03125
- a_gate: bfloat16 [64, 8192, 64], P('ad', 'tp'), may hold values from -0.0625 to 0.0625
- a_up: bfloat16 [64, 8192, 64], P('ad', 'tp'), may hold values from -0.0625 to 0.0625
- b_gate: bfloat16 [64, 64, 28672], P(None, 'tp', 'ad'), may hold values from -0.75 to 0.75
- b_up: bfloat16 [64, 64, 28672], P(None, 'tp', 'ad'), may hold values from -0.75 to 0.75
- a_down: bfloat16 [28672, 64, 64], P('ad', None, 'tp'), may hold values from -0.03125 to 0.03125
- b_down: bfloat16 [64, 64, 8192], P('ad', None, 'tp'), may hold values from -0.75 to 0.75
- adapter_ids: int32 [512, 1], replicated, may hold values from 0 to 63; in each aligned block of 512 rows (0 to 511, 512 to 1023, ...) at most 24 rows name the same one
- owner_map: int32 [64], replicated, may hold values from 0 to 63, each once
Outputs:
- mixed: bfloat16 [512, 8192], P('ad', 'tp')
The draws below stay inside these ranges and needn't reach their ends.
Inputs may be any that keep to these rules, and one draw needn't show every extreme that they name: `adapter_ids`: each row names one adapter; no adapter is named by more than 24 of the 512 rows, a bound that some block reaches. `owner_map`: each slot number appears once; slot k is held by index k of ad.
All inputs are finite; a program needn't handle non-finite values.
Results may differ from the reference program's by a relative error of at most 0.007.
Values may be sent and summed in bfloat16 or wider, within the bound.
No kernel may reach another device: no remote copies, remote signals or barrier semaphores. Data moves between devices by JAX's collectives and lax.ppermute only.
A program may use at most 64 MiB of HBM per device.

```python
import math
import jax
import jax.numpy as jnp
import numpy as np
from jax import lax

D = 8192
FF = 28672
RANK = 64
OCAP = 24
ROWS = 512
ADAPTERS = 64


def level_of(stream_key, extent, shards, least, top_value):
    gain = 1.0
    for dim, parts in shards:
        heights = jax.random.uniform(jax.random.fold_in(jax.random.fold_in(stream_key, 6), dim), (parts,), jnp.float32, least / len(shards), top_value / len(shards))
        gain = gain * jnp.repeat(jnp.exp(heights), extent[dim] // parts).reshape((-1,) + (1,) * (len(extent) - 1 - dim))
    return gain


def assign_block(key, own, number, rows, amount, top, most, skew):
    ranking = jax.random.permutation(key, amount)
    heavy_load, ordinary = shares(amount, rows * top, most, skew, True), shares(amount, rows * top, most, skew, False)
    places = jnp.arange(amount)

    def named(tallies, offset_by):
        used = int((tallies > 0).sum())
        fixed = max(1, used // 4)
        moved = fixed + (places - fixed + offset_by * (used - fixed)) % max(1, amount - fixed)
        return jnp.zeros((amount,), jnp.int32).at[ranking[jnp.where(places < fixed, places, moved)]].set(jnp.asarray(tallies, jnp.int32))

    tallies = jnp.where(number % 4 == 0, named(heavy_load, number // 4), named(ordinary, number - number // 4 - 1))
    mixed = jax.random.permutation(jax.random.fold_in(own, 3), amount)
    donor, sink = mixed[0:amount // 2 * 2:2], mixed[1:amount // 2 * 2:2]
    margin = jnp.minimum(tallies[donor] - 1, most - tallies[sink]) // 2
    margin = jnp.where((donor == ranking[0]) | (sink == ranking[0]) | (tallies[sink] == 0), 0, jnp.maximum(margin, 0))
    moved = jax.random.randint(jax.random.fold_in(own, 4), (amount // 2,), 0, 1 << 20) % (margin + 1)
    tallies = tallies.at[donor].add(-moved).at[sink].add(moved)
    items = jnp.searchsorted(jnp.cumsum(tallies), jnp.arange(rows * top), side="right").astype(jnp.int32)
    listing = items.reshape(top, rows).T
    listing = listing[jax.random.permutation(jax.random.fold_in(own, 1), rows)]
    offset_by = jax.random.randint(jax.random.fold_in(own, 2), (rows, 1), 0, top)
    return jnp.take_along_axis(listing, (jnp.arange(top)[None, :] + offset_by) % top, axis=1)


def shares(number_of, total, reach, slope, full):
    loads = [(1 << 20) // math.isqrt(standing ** slope) + 1 for standing in range(1, number_of + 1)]
    largest = reach if full else min(reach, max(-(-total // number_of), total * loads[0] // sum(loads)))
    least = 1 if total - largest >= number_of - 1 else 0
    given, rest = [largest] + [least] * (number_of - 1), total - largest - least * (number_of - 1)
    while rest > 0:
        candidates = [i for i in range(1, number_of) if given[i] < largest] or [i for i in range(1, number_of) if given[i] < reach]
        mass, left = sum([loads[i] for i in candidates]), rest
        for i in candidates:
            extra = min(reach - given[i], max(1, left * loads[i] // mass), rest)
            given[i] = given[i] + extra
            rest = rest - extra
    return np.array(given)


def gaussian(key, dims, width, bound, shards=(), dtype=jnp.bfloat16):
    entries = width * jax.random.normal(key, dims, jnp.float32)
    if shards:
        entries = entries * level_of(key, dims, shards, -0.22, 0.18)
    return jnp.clip(entries, -bound, bound).astype(dtype)


def setup_inputs(seed: int = 0) -> dict:
    streams_of = jax.random.split(jax.random.key(seed), 13)
    inputs = gaussian(streams_of[0], (ROWS, D), 1.0, 6.0, ((0, 64), (1, 8)))
    w_gate = gaussian(streams_of[1], (FF, D), D ** -0.5, 0.0625, ((0, 64), (1, 8)))
    w_up = gaussian(streams_of[2], (FF, D), D ** -0.5, 0.0625, ((0, 64), (1, 8)))
    w_down = gaussian(streams_of[3], (FF, D), FF ** -0.5, 0.03125, ((0, 64), (1, 8)))
    a_gate = gaussian(streams_of[4], (ADAPTERS, D, RANK), D ** -0.5, 0.0625, ((0, 64), (1, 8)))
    a_up = gaussian(streams_of[5], (ADAPTERS, D, RANK), D ** -0.5, 0.0625, ((0, 64), (1, 8)))
    b_gate = gaussian(streams_of[6], (ADAPTERS, RANK, FF), RANK ** -0.5, 0.75, ((1, 8), (2, 64)))
    b_up = gaussian(streams_of[7], (ADAPTERS, RANK, FF), RANK ** -0.5, 0.75, ((1, 8), (2, 64)))
    a_down = gaussian(streams_of[8], (FF, ADAPTERS, RANK), FF ** -0.5, 0.03125, ((0, 64), (2, 8)))
    b_down = gaussian(streams_of[9], (ADAPTERS, RANK, D), RANK ** -0.5, 0.75, ((0, 64), (2, 8)))
    adapter_ids_keys = jax.random.split(jax.random.fold_in(streams_of[10], 1), ROWS // ROWS)
    adapter_ids_turns = jax.random.permutation(jax.random.fold_in(streams_of[10], 3), ROWS // ROWS)
    adapter_ids = jax.vmap(lambda own, number: assign_block(jax.random.fold_in(streams_of[10], 2), own, number, ROWS, ADAPTERS, 1, OCAP, 2))(adapter_ids_keys, adapter_ids_turns).reshape((ROWS, 1))
    owner_map = jax.random.permutation(streams_of[11], ADAPTERS).astype(jnp.int32)
    return dict(inputs=inputs, w_gate=w_gate, w_up=w_up, w_down=w_down, a_gate=a_gate, a_up=a_up, b_gate=b_gate, b_up=b_up, a_down=a_down, b_down=b_down, adapter_ids=adapter_ids, owner_map=owner_map)


def reference(inputs, w_gate, w_up, w_down, a_gate, a_up, b_gate, b_up, a_down, b_down, adapter_ids, owner_map):
    slot = jnp.take(owner_map, adapter_ids[:, 0], axis=0).astype(jnp.int32)
    contract = (((1,), (1,)), ((), ()))

    def shrink(args):
        row, index = args
        gate_vec = jnp.dot(row[None, :], a_gate[index], preferred_element_type=jnp.float32)[0]
        up_vec = jnp.dot(row[None, :], a_up[index], preferred_element_type=jnp.float32)[0]
        return gate_vec, up_vec

    s_gate, s_up = lax.map(shrink, (inputs, slot))
    s_gate = s_gate.astype(jnp.bfloat16)
    s_up = s_up.astype(jnp.bfloat16)

    def expand(args):
        gate_low, up_low, index = args
        gate_vec = jnp.dot(gate_low[None, :], b_gate[index], preferred_element_type=jnp.float32)[0]
        up_vec = jnp.dot(up_low[None, :], b_up[index], preferred_element_type=jnp.float32)[0]
        return gate_vec, up_vec

    delta_gate, delta_up = lax.map(expand, (s_gate, s_up, slot))
    gate = lax.dot_general(inputs, w_gate, contract, preferred_element_type=jnp.float32) + delta_gate
    up = lax.dot_general(inputs, w_up, contract, preferred_element_type=jnp.float32) + delta_up
    hidden = (jax.nn.silu(gate) * up).astype(jnp.bfloat16)

    def shrink_down(args):
        row, index = args
        factor = lax.dynamic_index_in_dim(a_down, index, 1, keepdims=False)
        return jnp.dot(row[None, :], factor, preferred_element_type=jnp.float32)[0]

    shrunk_down = lax.map(shrink_down, (hidden, slot)).astype(jnp.bfloat16)

    def expand_down(args):
        low, index = args
        return jnp.dot(low[None, :], b_down[index], preferred_element_type=jnp.float32)[0]

    delta_down = lax.map(expand_down, (shrunk_down, slot))
    mixed = jnp.dot(hidden, w_down, preferred_element_type=jnp.float32) + delta_down
    return mixed.astype(jnp.bfloat16)
```

```python
import jax
import jax.numpy as jnp
from jax import lax
from jax.sharding import Mesh, PartitionSpec as P

OCAP = 24
F32 = jnp.float32
BF16 = jnp.bfloat16
NT = (((1,), (1,)), ((), ()))
TN = (((0,), (0,)), ((), ()))
OWN = ("x", "y", "c")
CHIPS = ("x", "y")


def spread(block, axes, count):
    copies = jnp.broadcast_to(block[None], (count,) + block.shape)
    return lax.all_to_all(copies, axes, 0, 0, tiled=True)


def per_device(
    inputs, w_gate, w_up, w_down, a_gate, a_up, b_gate, b_up, a_down, b_down, adapter_ids, owner_map
):
    chips = lax.axis_size("x") * lax.axis_size("y")
    cores = lax.axis_size("c")
    parts = lax.axis_size("z")
    owners = chips * cores
    here_owner = lax.axis_index(OWN)
    own_rows, width = inputs.shape
    rows = adapter_ids.shape[0]
    units = w_gate.shape[0]
    rank = a_gate.shape[2]
    rank_part = b_gate.shape[1]
    slots = owner_map.shape[0]

    half = spread(inputs, CHIPS, chips).reshape(chips * own_rows, width)
    piece = lax.all_gather(half, "c", axis=0, tiled=True)

    adapter = adapter_ids[:, 0].reshape(chips, cores, own_rows).transpose(1, 0, 2).reshape(rows)
    table = jnp.arange(slots, dtype=jnp.int32)
    row_slot = jnp.sum(jnp.where(adapter[:, None] == table[None, :], owner_map[None, :], 0), axis=1)
    onehot = (row_slot[:, None] == table[None, :]).astype(jnp.int32)
    position = jnp.sum((jnp.cumsum(onehot, axis=0) - onehot) * onehot, axis=1)
    place = row_slot * OCAP + position
    places = (place[:, None] == jnp.arange(slots * OCAP, dtype=jnp.int32)[None, :]).astype(BF16)
    mine = (
        place[:, None] == here_owner * OCAP + jnp.arange(OCAP, dtype=jnp.int32)[None, :]
    ).astype(BF16)
    slot_rows = (table[:, None] == row_slot[None, :]).astype(BF16)

    selected = lax.dot_general(mine, piece, TN, preferred_element_type=F32).astype(BF16)
    shrunk = jnp.stack(
        [
            jnp.dot(selected, a_gate[0], preferred_element_type=F32).reshape(OCAP, parts, rank_part),
            jnp.dot(selected, a_up[0], preferred_element_type=F32).reshape(OCAP, parts, rank_part),
        ],
        axis=2,
    )
    shrunk = shrunk.transpose(1, 0, 2, 3).reshape(parts, OCAP, 2 * rank_part).astype(BF16)
    shrunk = lax.all_to_all(shrunk, "z", 0, 0, tiled=True)
    shrunk = jnp.sum(shrunk.astype(F32), axis=0).astype(BF16)
    low_all = spread(shrunk, OWN, owners).reshape(owners * OCAP, 2 * rank_part)
    low_rows = lax.dot_general(
        low_all, places, (((0,), (1,)), ((), ())), preferred_element_type=F32
    ).astype(BF16)

    def expand(low, weights):
        wide = (slot_rows[:, None, :] * low[None, :, :]).reshape(slots * rank_part, rows)
        return lax.dot_general(
            weights.reshape(slots * rank_part, units), wide, TN, preferred_element_type=F32
        )

    gate_part = lax.dot_general(w_gate, piece, NT, preferred_element_type=F32) + expand(
        low_rows[:rank_part], b_gate
    )
    up_part = lax.dot_general(w_up, piece, NT, preferred_element_type=F32) + expand(
        low_rows[rank_part:], b_up
    )
    both = jnp.stack(
        [
            gate_part.astype(BF16).reshape(parts, units // parts, rows),
            up_part.astype(BF16).reshape(parts, units // parts, rows),
        ],
        axis=1,
    )
    both = lax.all_to_all(both, "z", 0, 0, tiled=True)
    both = jnp.sum(both.astype(F32), axis=0)
    hidden = (jax.nn.silu(both[0]) * both[1]).astype(BF16)
    hidden_all = spread(hidden, "z", parts).reshape(units, rows)

    rank_full = lax.dot_general(
        a_down.reshape(units, slots * rank_part), hidden_all, TN, preferred_element_type=F32
    )
    rank_rows = jnp.sum(
        rank_full.reshape(slots, rank_part, rows) * slot_rows.astype(F32)[:, None, :], axis=0
    ).astype(BF16)
    rank_sent = lax.dot_general(
        places, rank_rows, (((0,), (1,)), ((), ())), preferred_element_type=F32
    ).astype(BF16)
    rank_sum = lax.all_to_all(
        rank_sent.reshape(owners, OCAP, rank_part), OWN, 0, 0, tiled=True
    )
    rank_sum = jnp.sum(rank_sum.astype(F32), axis=0).astype(BF16)
    rank_all = spread(rank_sum, "z", parts).transpose(1, 0, 2).reshape(OCAP, rank)
    rank_mine = jnp.dot(mine, rank_all, preferred_element_type=F32).astype(BF16)
    out = lax.dot_general(hidden_all, w_down, TN, preferred_element_type=F32) + jnp.dot(
        rank_mine, b_down[0], preferred_element_type=F32
    )
    out = out.astype(BF16).reshape(cores, chips, own_rows, width)
    out = lax.all_to_all(out, "c", 0, 0, tiled=True)
    out = jnp.sum(out.astype(F32), axis=0).astype(BF16)
    out = lax.all_to_all(out, CHIPS, 0, 0, tiled=True)
    return jnp.sum(out.astype(F32), axis=0).astype(BF16)


def solution(mesh):
    side = (4, 8, 2, 8)
    fine = Mesh(mesh.devices.reshape(side), ("x", "y", "c", "z"))
    ad, tp = ("x", "y", "c"), "z"
    placed = (
        P(ad, tp),
        P(ad, tp),
        P(ad, tp),
        P(ad, tp),
        P(ad, tp, None),
        P(ad, tp, None),
        P(None, tp, ad),
        P(None, tp, ad),
        P(ad, None, tp),
        P(ad, None, tp),
        P(),
        P(),
    )
    return jax.shard_map(
        per_device, mesh=fine, in_specs=placed, out_specs=P(ad, tp), check_vma=False
    )
```

```python
import jax
import jax.numpy as jnp
from jax import lax
from jax.sharding import Mesh, PartitionSpec as P

OCAP = 24
F32 = jnp.float32
BF16 = jnp.bfloat16
NT = (((1,), (1,)), ((), ()))
TN = (((0,), (0,)), ((), ()))
OWN = ("x", "y", "c")
CHIPS = ("x", "y")


def spread(block, axes, count):
    copies = jnp.broadcast_to(block[None], (count,) + block.shape)
    return lax.all_to_all(copies, axes, 0, 0, tiled=True)


def per_device(
    inputs, w_gate, w_up, w_down, a_gate, a_up, b_gate, b_up, a_down, b_down, adapter_ids, owner_map
):
    chips = lax.axis_size("x") * lax.axis_size("y")
    cores = lax.axis_size("c")
    parts = lax.axis_size("z")
    owners = chips * cores
    here_owner = lax.axis_index(OWN)
    own_rows, width = inputs.shape
    rows = adapter_ids.shape[0]
    units = w_gate.shape[0]
    rank = a_gate.shape[2]
    rank_part = b_gate.shape[1]
    slots = owner_map.shape[0]

    swap = [(0, 1), (1, 0)]
    half = spread(inputs, CHIPS, chips).reshape(chips * own_rows, width)
    piece = jnp.concatenate([half, lax.ppermute(half, "c", swap)], axis=0)

    adapter = adapter_ids[:, 0]
    table = jnp.arange(slots, dtype=jnp.int32)
    row_slot = jnp.sum(jnp.where(adapter[:, None] == table[None, :], owner_map[None, :], 0), axis=1)
    onehot = (row_slot[:, None] == table[None, :]).astype(jnp.int32)
    position = jnp.sum((jnp.cumsum(onehot, axis=0) - onehot) * onehot, axis=1)
    place = row_slot * OCAP + position

    def ordered(values):
        by_core = values.reshape(chips, cores, own_rows).transpose(1, 0, 2)
        by_core = by_core.reshape(cores, chips * own_rows)
        return jnp.where(lax.axis_index("c") == 0, by_core, by_core[::-1]).reshape(rows)

    row_slot, place = ordered(row_slot), ordered(place)
    places = (place[:, None] == jnp.arange(slots * OCAP, dtype=jnp.int32)[None, :]).astype(BF16)
    mine = (
        place[:, None] == here_owner * OCAP + jnp.arange(OCAP, dtype=jnp.int32)[None, :]
    ).astype(BF16)
    slot_rows = (table[:, None] == row_slot[None, :]).astype(BF16)

    selected = lax.dot_general(mine, piece, TN, preferred_element_type=F32).astype(BF16)
    shrunk = jnp.stack(
        [
            jnp.dot(selected, a_gate[0], preferred_element_type=F32).reshape(OCAP, parts, rank_part),
            jnp.dot(selected, a_up[0], preferred_element_type=F32).reshape(OCAP, parts, rank_part),
        ],
        axis=2,
    )
    shrunk = shrunk.transpose(1, 0, 2, 3).reshape(parts, OCAP, 2 * rank_part).astype(BF16)
    shrunk = lax.all_to_all(shrunk, "z", 0, 0, tiled=True)
    shrunk = jnp.sum(shrunk.astype(F32), axis=0).astype(BF16)
    low_all = spread(shrunk, OWN, owners).reshape(owners * OCAP, 2 * rank_part)
    low_rows = lax.dot_general(
        low_all, places, (((0,), (1,)), ((), ())), preferred_element_type=F32
    ).astype(BF16)

    def expand(low, weights):
        wide = (slot_rows[:, None, :] * low[None, :, :]).reshape(slots * rank_part, rows)
        return lax.dot_general(
            weights.reshape(slots * rank_part, units), wide, TN, preferred_element_type=F32
        )

    gate_part = lax.dot_general(w_gate, piece, NT, preferred_element_type=F32) + expand(
        low_rows[:rank_part], b_gate
    )
    up_part = lax.dot_general(w_up, piece, NT, preferred_element_type=F32) + expand(
        low_rows[rank_part:], b_up
    )
    both = jnp.stack(
        [
            gate_part.astype(BF16).reshape(parts, units // parts, rows),
            up_part.astype(BF16).reshape(parts, units // parts, rows),
        ],
        axis=1,
    )
    both = lax.all_to_all(both, "z", 0, 0, tiled=True)
    both = jnp.sum(both.astype(F32), axis=0)
    hidden = (jax.nn.silu(both[0]) * both[1]).astype(BF16)
    hidden_all = spread(hidden, "z", parts).reshape(units, rows)

    rank_full = lax.dot_general(
        a_down.reshape(units, slots * rank_part), hidden_all, TN, preferred_element_type=F32
    )
    rank_rows = jnp.sum(
        rank_full.reshape(slots, rank_part, rows) * slot_rows.astype(F32)[:, None, :], axis=0
    ).astype(BF16)
    rank_sent = lax.dot_general(
        places, rank_rows, (((0,), (1,)), ((), ())), preferred_element_type=F32
    ).astype(BF16)
    rank_sum = lax.all_to_all(
        rank_sent.reshape(owners, OCAP, rank_part), OWN, 0, 0, tiled=True
    )
    rank_sum = jnp.sum(rank_sum.astype(F32), axis=0).astype(BF16)
    rank_all = spread(rank_sum, "z", parts).transpose(1, 0, 2).reshape(OCAP, rank)
    rank_mine = jnp.dot(mine, rank_all, preferred_element_type=F32).astype(BF16)
    out = lax.dot_general(hidden_all, w_down, TN, preferred_element_type=F32) + jnp.dot(
        rank_mine, b_down[0], preferred_element_type=F32
    )
    kept, given = out[: rows // cores], out[rows // cores :].astype(BF16)
    out = (kept + lax.ppermute(given, "c", swap).astype(F32)).astype(BF16)
    out = lax.all_to_all(out.reshape(chips, own_rows, width), CHIPS, 0, 0, tiled=True)
    return jnp.sum(out.astype(F32), axis=0).astype(BF16)


def solution(mesh):
    side = (4, 8, 2, 8)
    fine = Mesh(mesh.devices.reshape(side), ("x", "y", "c", "z"))
    ad, tp = ("x", "y", "c"), "z"
    placed = (
        P(ad, tp),
        P(ad, tp),
        P(ad, tp),
        P(ad, tp),
        P(ad, tp, None),
        P(ad, tp, None),
        P(None, tp, ad),
        P(None, tp, ad),
        P(ad, None, tp),
        P(ad, None, tp),
        P(),
        P(),
    )
    return jax.shard_map(
        per_device, mesh=fine, in_specs=placed, out_specs=P(ad, tp), check_vma=False
    )
```

```python
import jax
import jax.numpy as jnp
from jax import lax
from jax.sharding import Mesh, PartitionSpec as P

OCAP = 24
LANES = 128
F32 = jnp.float32
BF16 = jnp.bfloat16
NT = (((1,), (1,)), ((), ()))
TN = (((0,), (0,)), ((), ()))
OWN = ("x", "y", "c")
CHIPS = ("x", "y")


def spread(block, axes, count):
    copies = jnp.broadcast_to(block[None], (count,) + block.shape)
    return lax.all_to_all(copies, axes, 0, 0, tiled=True)


def per_device(
    inputs, w_gate, w_up, w_down, a_gate, a_up, b_gate, b_up, a_down, b_down, adapter_ids, owner_map
):
    chips = lax.axis_size("x") * lax.axis_size("y")
    cores = lax.axis_size("c")
    parts = lax.axis_size("z")
    owners = chips * cores
    here_owner = lax.axis_index(OWN)
    own_rows, width = inputs.shape
    rows = adapter_ids.shape[0]
    units = w_gate.shape[0]
    rank = a_gate.shape[2]
    rank_part = b_gate.shape[1]
    slots = owner_map.shape[0]

    down_shrink = lax.all_gather(a_down.reshape(units, slots * rank_part), "z", axis=0)
    down_expand = lax.all_gather(b_down[0], OWN, axis=0)

    swap = [(0, 1), (1, 0)]
    half = spread(inputs, CHIPS, chips).reshape(chips * own_rows, width)
    piece = jnp.concatenate([half, lax.ppermute(half, "c", swap)], axis=0)

    adapter = adapter_ids[:, 0]
    table = jnp.arange(slots, dtype=jnp.int32)
    row_slot = jnp.sum(jnp.where(adapter[:, None] == table[None, :], owner_map[None, :], 0), axis=1)
    onehot = (row_slot[:, None] == table[None, :]).astype(jnp.int32)
    position = jnp.sum((jnp.cumsum(onehot, axis=0) - onehot) * onehot, axis=1)
    place = row_slot * OCAP + position

    def ordered(values):
        by_core = values.reshape(chips, cores, own_rows).transpose(1, 0, 2)
        by_core = by_core.reshape(cores, chips * own_rows)
        return jnp.where(lax.axis_index("c") == 0, by_core, by_core[::-1]).reshape(rows)

    row_slot_all = row_slot
    row_slot, place = ordered(row_slot), ordered(place)
    places = (place[:, None] == jnp.arange(slots * OCAP, dtype=jnp.int32)[None, :]).astype(BF16)
    mine = (
        place[:, None] == here_owner * OCAP + jnp.arange(OCAP, dtype=jnp.int32)[None, :]
    ).astype(BF16)
    slot_rows = (table[:, None] == row_slot[None, :]).astype(BF16)

    selected = lax.dot_general(mine, piece, TN, preferred_element_type=F32).astype(BF16)
    shrunk = jnp.stack(
        [
            jnp.dot(selected, a_gate[0], preferred_element_type=F32).reshape(OCAP, parts, rank_part),
            jnp.dot(selected, a_up[0], preferred_element_type=F32).reshape(OCAP, parts, rank_part),
        ],
        axis=2,
    )
    shrunk = shrunk.transpose(1, 0, 2, 3).reshape(parts, OCAP, 2 * rank_part).astype(BF16)
    shrunk = lax.all_to_all(shrunk, "z", 0, 0, tiled=True)
    shrunk = jnp.sum(shrunk.astype(F32), axis=0).astype(BF16)
    low_all = spread(shrunk, OWN, owners)
    gate_base = lax.dot_general(w_gate, piece, NT, preferred_element_type=F32)
    up_base = lax.dot_general(w_up, piece, NT, preferred_element_type=F32)
    low_all, gate_base, up_base = lax.optimization_barrier((low_all, gate_base, up_base))
    low_all = low_all.reshape(owners * OCAP, 2 * rank_part)
    low_rows = lax.dot_general(
        low_all, places, (((0,), (1,)), ((), ())), preferred_element_type=F32
    ).astype(BF16)

    def expand(low, weights):
        wide = (slot_rows[:, None, :] * low[None, :, :]).reshape(slots * rank_part, rows)
        return lax.dot_general(
            weights.reshape(slots * rank_part, units), wide, TN, preferred_element_type=F32
        )

    gate_part = gate_base + expand(low_rows[:rank_part], b_gate)
    up_part = up_base + expand(low_rows[rank_part:], b_up)
    both = jnp.stack(
        [
            gate_part.astype(BF16).reshape(parts, units // parts, rows),
            up_part.astype(BF16).reshape(parts, units // parts, rows),
        ],
        axis=1,
    )
    both = lax.all_to_all(both, "z", 0, 0, tiled=True)
    both = jnp.sum(both.astype(F32), axis=0)
    hidden = (jax.nn.silu(both[0]) * both[1]).astype(BF16)
    hidden_all = spread(hidden, "z", parts).reshape(units, rows)

    slot_mask = slot_rows.astype(F32)[:, None, :]

    def shrink(block):
        full = lax.dot_general(block, hidden_all, TN, preferred_element_type=F32)
        return jnp.sum(full.reshape(slots, rank_part, rows) * slot_mask, axis=0)

    low_width = -(-rank // LANES) * LANES
    low = jnp.concatenate([shrink(down_shrink[k]) for k in range(parts)], axis=0).astype(BF16)
    low = lax.dot_general(low, jnp.eye(rank, low_width, dtype=BF16), TN, preferred_element_type=F32)
    out = lax.dot_general(hidden_all, w_down, TN, preferred_element_type=F32)
    out = jnp.concatenate([out, low], axis=1)
    kept, given = out[: rows // cores], out[rows // cores :].astype(BF16)
    out = (kept + lax.ppermute(given, "c", swap).astype(F32)).astype(BF16)
    out = lax.all_to_all(out.reshape(chips, own_rows, width + low_width), CHIPS, 0, 0, tiled=True)
    out = jnp.sum(out.astype(F32), axis=0)
    low = out[:, width : width + rank].astype(BF16)
    own_slot = lax.dynamic_slice(row_slot_all, (here_owner * own_rows,), (own_rows,))
    own_hot = (own_slot[:, None] == table[None, :]).astype(BF16)
    wide = (own_hot[:, :, None] * low[:, None, :]).reshape(own_rows, slots * rank)
    delta = jnp.dot(
        wide, down_expand.reshape(slots * rank, width), preferred_element_type=F32
    )
    return (out[:, :width] + delta).astype(BF16)


def solution(mesh):
    side = (4, 8, 2, 8)
    fine = Mesh(mesh.devices.reshape(side), ("x", "y", "c", "z"))
    ad, tp = ("x", "y", "c"), "z"
    placed = (
        P(ad, tp),
        P(ad, tp),
        P(ad, tp),
        P(ad, tp),
        P(ad, tp, None),
        P(ad, tp, None),
        P(None, tp, ad),
        P(None, tp, ad),
        P(ad, None, tp),
        P(ad, None, tp),
        P(),
        P(),
    )
    return jax.shard_map(
        per_device, mesh=fine, in_specs=placed, out_specs=P(ad, tp), check_vma=False
    )
```

```python
import jax
import jax.numpy as jnp
from jax import lax
from jax.sharding import Mesh, PartitionSpec as P

OCAP = 24
LANES = 128
F32 = jnp.float32
BF16 = jnp.bfloat16
NT = (((1,), (1,)), ((), ()))
TN = (((0,), (0,)), ((), ()))
OWN = ("x", "y", "c")
CHIPS = ("x", "y")


def spread(block, axes, count):
    copies = jnp.broadcast_to(block[None], (count,) + block.shape)
    return lax.all_to_all(copies, axes, 0, 0, tiled=True)


def per_device(
    inputs, w_gate, w_up, w_down, a_gate, a_up, b_gate, b_up, a_down, b_down, adapter_ids, owner_map
):
    chips = lax.axis_size("x") * lax.axis_size("y")
    cores = lax.axis_size("c")
    parts = lax.axis_size("z")
    owners = chips * cores
    here_owner = lax.axis_index(OWN)
    own_rows, width = inputs.shape
    rows = adapter_ids.shape[0]
    units = w_gate.shape[0]
    rank = a_gate.shape[2]
    rank_part = b_gate.shape[1]
    slots = owner_map.shape[0]

    swap = [(0, 1), (1, 0)]
    half = spread(inputs, CHIPS, chips)
    down_other = lax.ppermute(b_down[0], "c", swap)
    half, down_other = lax.optimization_barrier((half, down_other))
    half = half.reshape(chips * own_rows, width)
    piece = jnp.concatenate([half, lax.ppermute(half, "c", swap)], axis=0)

    adapter = adapter_ids[:, 0]
    table = jnp.arange(slots, dtype=jnp.int32)
    row_slot = jnp.sum(jnp.where(adapter[:, None] == table[None, :], owner_map[None, :], 0), axis=1)
    onehot = (row_slot[:, None] == table[None, :]).astype(jnp.int32)
    position = jnp.sum((jnp.cumsum(onehot, axis=0) - onehot) * onehot, axis=1)

    def ordered(values):
        by_core = values.reshape(chips, cores, own_rows).transpose(1, 0, 2)
        by_core = by_core.reshape(cores, chips * own_rows)
        return jnp.where(lax.axis_index("c") == 0, by_core, by_core[::-1]).reshape(rows)

    row_slot, position = ordered(row_slot), ordered(position)
    up_per = LANES // (2 * rank_part)
    up_lines = OCAP // up_per
    place_of = jnp.arange(OCAP, dtype=jnp.int32)
    mine = ((row_slot == here_owner)[:, None] & (position[:, None] == place_of[None, :])).astype(BF16)
    up_line = row_slot * up_lines + position // up_per
    up_lines_all = jnp.arange(slots * up_lines, dtype=jnp.int32)
    up_pick = (up_line[:, None] == up_lines_all[None, :]).astype(BF16)
    lane = jnp.arange(LANES, dtype=jnp.int32)
    up_lane = lane[:, None] // (2 * rank_part) == (position % up_per)[None, :]
    half_rows = chips * own_rows
    here_core = lax.axis_index("c")
    row_core = jnp.where(jnp.arange(rows) < half_rows, here_core, 1 - here_core)
    apart = (row_slot % cores) ^ row_core
    down_per = LANES // rank_part
    down_lines = cores * OCAP // down_per
    seat = apart * OCAP + position
    down_line = (row_slot - row_slot % cores + row_core) * down_lines + seat // down_per
    down_lines_all = jnp.arange(owners * down_lines, dtype=jnp.int32)
    down_pick = (down_lines_all[:, None] == down_line[None, :]).astype(BF16)
    down_seat = jnp.arange(down_per, dtype=jnp.int32)[:, None] == (seat % down_per)[None, :]
    down_seat = down_seat.astype(BF16)[:, None, :]
    our_line = down_line[:half_rows, None] - here_owner * down_lines
    ours = (our_line == jnp.arange(down_lines, dtype=jnp.int32)[None, :]).astype(BF16)
    our_seat = (seat % down_per)[:half_rows, None] == (lane // rank_part)[None, :]
    our_slot = [(apart[:half_rows, None] == u).astype(BF16) for u in range(cores)]
    slot_rows = (table[:, None] == row_slot[None, :]).astype(BF16)

    selected = lax.dot_general(mine, piece, TN, preferred_element_type=F32).astype(BF16)
    shrunk = jnp.concatenate(
        [
            jnp.dot(selected, a_gate[0], preferred_element_type=F32),
            jnp.dot(selected, a_up[0], preferred_element_type=F32),
        ],
        axis=1,
    ).astype(BF16)
    column = jnp.arange(parts * LANES, dtype=jnp.int32)
    part, seat_up = column // LANES, column % LANES // (2 * rank_part)
    low = column % (2 * rank_part)
    source = part * rank_part + low % rank_part + low // rank_part * rank
    move = (jnp.arange(2 * rank, dtype=jnp.int32)[:, None] == source[None, :]).astype(BF16)
    shrunk = jnp.dot(shrunk, move, preferred_element_type=F32)
    shrunk = jnp.where(place_of[:, None] % up_per == seat_up[None, :], shrunk, 0).astype(BF16)
    line_of = jnp.arange(up_lines, dtype=jnp.int32)[:, None] == place_of[None, :] // up_per
    shrunk = jnp.dot(line_of.astype(BF16), shrunk, preferred_element_type=F32).astype(BF16)
    shrunk = shrunk.reshape(up_lines, parts, LANES).transpose(1, 0, 2)
    shrunk = lax.all_to_all(shrunk, "z", 0, 0, tiled=True)
    shrunk = jnp.sum(shrunk.astype(F32), axis=0).astype(BF16)
    low_all = spread(shrunk, OWN, owners)
    gate_base = lax.dot_general(w_gate, piece, NT, preferred_element_type=F32)
    up_base = lax.dot_general(w_up, piece, NT, preferred_element_type=F32)
    low_all, gate_base, up_base = lax.optimization_barrier((low_all, gate_base, up_base))
    low_rows = lax.dot_general(
        low_all.reshape(slots * up_lines, LANES),
        up_pick,
        (((0,), (1,)), ((), ())),
        preferred_element_type=F32,
    )
    low_rows = jnp.where(up_lane, low_rows, 0).reshape(up_per, 2 * rank_part, rows)
    low_rows = jnp.sum(low_rows, axis=0).astype(BF16)

    def expand(low, weights):
        wide = (slot_rows[:, None, :] * low[None, :, :]).reshape(slots * rank_part, rows)
        return lax.dot_general(
            weights.reshape(slots * rank_part, units), wide, TN, preferred_element_type=F32
        )

    gate_part = gate_base + expand(low_rows[:rank_part], b_gate)
    up_part = up_base + expand(low_rows[rank_part:], b_up)
    both = jnp.stack(
        [
            gate_part.astype(BF16).reshape(parts, units // parts, rows),
            up_part.astype(BF16).reshape(parts, units // parts, rows),
        ],
        axis=1,
    )
    both = lax.all_to_all(both, "z", 0, 0, tiled=True)
    both = jnp.sum(both.astype(F32), axis=0)
    hidden = (jax.nn.silu(both[0]) * both[1]).astype(BF16)
    hidden_all = spread(hidden, "z", parts).reshape(units, rows)

    rank_full = lax.dot_general(
        a_down.reshape(units, slots * rank_part), hidden_all, TN, preferred_element_type=F32
    )
    rank_rows = jnp.sum(
        rank_full.reshape(slots, rank_part, rows) * slot_rows.astype(F32)[:, None, :], axis=0
    ).astype(BF16)
    rank_wide = (down_seat * rank_rows[None, :, :]).reshape(LANES, rows)
    rank_sent = lax.dot_general(down_pick, rank_wide, NT, preferred_element_type=F32).astype(BF16)
    rank_sum = lax.all_to_all(
        rank_sent.reshape(owners, down_lines, LANES), OWN, 0, 0, tiled=True
    )
    out = lax.dot_general(hidden_all, w_down, TN, preferred_element_type=F32)
    rank_sum, out = lax.optimization_barrier((rank_sum, out))
    rank_sum = jnp.sum(rank_sum.astype(F32), axis=0).astype(BF16)
    rank_all = spread(rank_sum, "z", parts)
    kept, given = out[:half_rows], out[half_rows:].astype(BF16)
    out = kept + lax.ppermute(given, "c", swap).astype(F32)
    rank_all, out = lax.optimization_barrier((rank_all, out))
    rank_ours = lax.dot_general(
        ours, rank_all, (((1,), (1,)), ((), ())), preferred_element_type=F32
    )
    rank_ours = jnp.where(our_seat[:, None, :], rank_ours, 0).astype(BF16)
    gathered = column // LANES * rank_part + column % rank_part
    fold = (gathered[:, None] == jnp.arange(rank, dtype=jnp.int32)[None, :]).astype(BF16)
    rank_ours = jnp.dot(
        rank_ours.reshape(half_rows, parts * LANES), fold, preferred_element_type=F32
    ).astype(BF16)
    for in_slot, factor in zip(our_slot, (b_down[0], down_other)):
        out = out + jnp.dot(rank_ours * in_slot, factor, preferred_element_type=F32)
    out = out.astype(BF16)
    out = lax.all_to_all(out.reshape(chips, own_rows, width), CHIPS, 0, 0, tiled=True)
    return jnp.sum(out.astype(F32), axis=0).astype(BF16)


def solution(mesh):
    side = (4, 8, 2, 8)
    fine = Mesh(mesh.devices.reshape(side), ("x", "y", "c", "z"))
    ad, tp = ("x", "y", "c"), "z"
    placed = (
        P(ad, tp),
        P(ad, tp),
        P(ad, tp),
        P(ad, tp),
        P(ad, tp, None),
        P(ad, tp, None),
        P(None, tp, ad),
        P(None, tp, ad),
        P(ad, None, tp),
        P(ad, None, tp),
        P(),
        P(),
    )
    return jax.shard_map(
        per_device, mesh=fine, in_specs=placed, out_specs=P(ad, tp), check_vma=False
    )
```

```python
import jax
import jax.numpy as jnp
from jax import lax
from jax.sharding import Mesh, PartitionSpec as P

OCAP = 24
LANES = 128
F32 = jnp.float32
BF16 = jnp.bfloat16
NT = (((1,), (1,)), ((), ()))
TN = (((0,), (0,)), ((), ()))
OWN = ("x", "y", "c")
CHIPS = ("x", "y")


def spread(block, axes, count):
    copies = jnp.broadcast_to(block[None], (count,) + block.shape)
    return lax.all_to_all(copies, axes, 0, 0, tiled=True)


def per_device(
    inputs, w_gate, w_up, w_down, a_gate, a_up, b_gate, b_up, a_down, b_down, adapter_ids, owner_map
):
    chips = lax.axis_size("x") * lax.axis_size("y")
    cores = lax.axis_size("c")
    parts = lax.axis_size("z")
    owners = chips * cores
    here_owner = lax.axis_index(OWN)
    own_rows, width = inputs.shape
    rows = adapter_ids.shape[0]
    units = w_gate.shape[0]
    rank = a_gate.shape[2]
    rank_part = b_gate.shape[1]
    slots = owner_map.shape[0]

    swap = [(0, 1), (1, 0)]
    half = spread(inputs, CHIPS, chips)
    down_other = lax.ppermute(b_down[0], "c", swap)
    half, down_other = lax.optimization_barrier((half, down_other))
    half = half.reshape(chips * own_rows, width)
    piece = jnp.concatenate([half, lax.ppermute(half, "c", swap)], axis=0)

    adapter = adapter_ids[:, 0]
    table = jnp.arange(slots, dtype=jnp.int32)
    row_slot = jnp.sum(jnp.where(adapter[:, None] == table[None, :], owner_map[None, :], 0), axis=1)
    onehot = (row_slot[:, None] == table[None, :]).astype(jnp.int32)
    position = jnp.sum((jnp.cumsum(onehot, axis=0) - onehot) * onehot, axis=1)

    def ordered(values):
        by_core = values.reshape(chips, cores, own_rows).transpose(1, 0, 2)
        by_core = by_core.reshape(cores, chips * own_rows)
        return jnp.where(lax.axis_index("c") == 0, by_core, by_core[::-1]).reshape(rows)

    row_slot, position = ordered(row_slot), ordered(position)
    up_per = LANES // (2 * rank_part)
    up_lines = OCAP // up_per
    place_of = jnp.arange(OCAP, dtype=jnp.int32)
    mine = ((row_slot == here_owner)[:, None] & (position[:, None] == place_of[None, :])).astype(BF16)
    up_line = row_slot * up_lines + position // up_per
    up_lines_all = jnp.arange(slots * up_lines, dtype=jnp.int32)
    up_pick = (up_line[:, None] == up_lines_all[None, :]).astype(BF16)
    lane = jnp.arange(LANES, dtype=jnp.int32)
    up_lane = lane[:, None] // (2 * rank_part) == (position % up_per)[None, :]
    half_rows = chips * own_rows
    here_core = lax.axis_index("c")
    row_core = jnp.where(jnp.arange(rows) < half_rows, here_core, 1 - here_core)
    apart = (row_slot % cores) ^ row_core
    down_per = LANES // rank_part
    down_lines = cores * OCAP // down_per
    seat = apart * OCAP + position
    down_line = (row_slot - row_slot % cores + row_core) * down_lines + seat // down_per
    down_lines_all = jnp.arange(owners * down_lines, dtype=jnp.int32)
    down_pick = (down_lines_all[:, None] == down_line[None, :]).astype(BF16)
    down_seat = jnp.arange(down_per, dtype=jnp.int32)[:, None] == (seat % down_per)[None, :]
    down_seat = down_seat.astype(BF16)[:, None, :]
    our_line = down_line[:half_rows, None] - here_owner * down_lines
    ours = (our_line == jnp.arange(down_lines, dtype=jnp.int32)[None, :]).astype(BF16)
    our_seat = (seat % down_per)[:half_rows, None] == (lane // rank_part)[None, :]
    our_slot = [(apart[:half_rows, None] == u).astype(BF16) for u in range(cores)]
    slot_rows = (table[:, None] == row_slot[None, :]).astype(BF16)

    selected = lax.dot_general(mine, piece, TN, preferred_element_type=F32).astype(BF16)
    shrunk = jnp.concatenate(
        [
            jnp.dot(selected, a_gate[0], preferred_element_type=F32),
            jnp.dot(selected, a_up[0], preferred_element_type=F32),
        ],
        axis=1,
    ).astype(BF16)
    column = jnp.arange(parts * LANES, dtype=jnp.int32)
    part, seat_up = column // LANES, column % LANES // (2 * rank_part)
    low = column % (2 * rank_part)
    source = part * rank_part + low % rank_part + low // rank_part * rank
    move = (jnp.arange(2 * rank, dtype=jnp.int32)[:, None] == source[None, :]).astype(BF16)
    shrunk = jnp.dot(shrunk, move, preferred_element_type=F32)
    shrunk = jnp.where(place_of[:, None] % up_per == seat_up[None, :], shrunk, 0).astype(BF16)
    line_of = jnp.arange(up_lines, dtype=jnp.int32)[:, None] == place_of[None, :] // up_per
    shrunk = jnp.dot(line_of.astype(BF16), shrunk, preferred_element_type=F32).astype(BF16)
    shrunk = shrunk.reshape(up_lines, parts, LANES).transpose(1, 0, 2)
    shrunk = lax.all_to_all(shrunk, "z", 0, 0, tiled=True)
    shrunk = jnp.sum(shrunk.astype(F32), axis=0).astype(BF16)
    low_all = spread(shrunk, OWN, owners)
    gate_base = lax.dot_general(w_gate, piece, NT, preferred_element_type=F32)
    up_base = lax.dot_general(w_up, piece, NT, preferred_element_type=F32)
    masks = (down_pick, down_seat, ours, our_seat, *our_slot)
    low_all, gate_base, up_base, masks = lax.optimization_barrier(
        (low_all, gate_base, up_base, masks)
    )
    down_pick, down_seat, ours, our_seat, *our_slot = masks
    low_rows = lax.dot_general(
        low_all.reshape(slots * up_lines, LANES),
        up_pick,
        (((0,), (1,)), ((), ())),
        preferred_element_type=F32,
    )
    low_rows = jnp.where(up_lane, low_rows, 0).astype(BF16)
    gather_up = jnp.arange(2 * rank_part, dtype=jnp.int32)[:, None] == lane[None, :] % (2 * rank_part)
    low_rows = jnp.dot(gather_up.astype(BF16), low_rows, preferred_element_type=F32).astype(BF16)

    def expand(low, weights):
        wide = (slot_rows[:, None, :] * low[None, :, :]).reshape(slots * rank_part, rows)
        return lax.dot_general(
            weights.reshape(slots * rank_part, units), wide, TN, preferred_element_type=F32
        )

    gate_part = gate_base + expand(low_rows[:rank_part], b_gate)
    up_part = up_base + expand(low_rows[rank_part:], b_up)
    both = jnp.stack(
        [
            gate_part.astype(BF16).reshape(parts, units // parts, rows),
            up_part.astype(BF16).reshape(parts, units // parts, rows),
        ],
        axis=1,
    )
    both = lax.all_to_all(both, "z", 0, 0, tiled=True)
    both = jnp.sum(both.astype(F32), axis=0)
    hidden = (jax.nn.silu(both[0]) * both[1]).astype(BF16)
    hidden_all = spread(hidden, "z", parts).reshape(units, rows)

    rank_full = lax.dot_general(
        a_down.reshape(units, slots * rank_part), hidden_all, TN, preferred_element_type=F32
    )
    rank_rows = jnp.sum(
        rank_full.reshape(slots, rank_part, rows) * slot_rows.astype(F32)[:, None, :], axis=0
    ).astype(BF16)
    rank_wide = (down_seat * rank_rows[None, :, :]).reshape(LANES, rows)
    rank_sent = lax.dot_general(down_pick, rank_wide, NT, preferred_element_type=F32).astype(BF16)
    rank_sum = lax.all_to_all(
        rank_sent.reshape(owners, down_lines, LANES), OWN, 0, 0, tiled=True
    )
    out = lax.dot_general(hidden_all, w_down, TN, preferred_element_type=F32)
    kept, given = out[:half_rows], out[half_rows:].astype(BF16)
    rank_sum, kept, given = lax.optimization_barrier((rank_sum, kept, given))
    rank_sum = jnp.sum(rank_sum.astype(F32), axis=0).astype(BF16)
    rank_all = spread(rank_sum, "z", parts)
    out = kept + lax.ppermute(given, "c", swap).astype(F32)
    rank_ours = lax.dot_general(
        ours, rank_all, (((1,), (1,)), ((), ())), preferred_element_type=F32
    )
    rank_ours = jnp.where(our_seat[:, None, :], rank_ours, 0).astype(BF16)
    gathered = column // LANES * rank_part + column % rank_part
    fold = (gathered[:, None] == jnp.arange(rank, dtype=jnp.int32)[None, :]).astype(BF16)
    rank_ours = jnp.dot(
        rank_ours.reshape(half_rows, parts * LANES), fold, preferred_element_type=F32
    ).astype(BF16)
    for in_slot, factor in zip(our_slot, (b_down[0], down_other)):
        out = out + jnp.dot(rank_ours * in_slot, factor, preferred_element_type=F32)
    out = out.astype(BF16)
    out = lax.all_to_all(out.reshape(chips, own_rows, width), CHIPS, 0, 0, tiled=True)
    return jnp.sum(out.astype(F32), axis=0).astype(BF16)


def solution(mesh):
    side = (4, 8, 2, 8)
    fine = Mesh(mesh.devices.reshape(side), ("x", "y", "c", "z"))
    ad, tp = ("x", "y", "c"), "z"
    placed = (
        P(ad, tp),
        P(ad, tp),
        P(ad, tp),
        P(ad, tp),
        P(ad, tp, None),
        P(ad, tp, None),
        P(None, tp, ad),
        P(None, tp, ad),
        P(ad, None, tp),
        P(ad, None, tp),
        P(),
        P(),
    )
    return jax.shard_map(
        per_device, mesh=fine, in_specs=placed, out_specs=P(ad, tp), check_vma=False
    )
```

```python
import jax
import jax.numpy as jnp
from jax import lax
from jax.sharding import Mesh, PartitionSpec as P

OCAP = 24
LANES = 128
F32 = jnp.float32
BF16 = jnp.bfloat16
NT = (((1,), (1,)), ((), ()))
TN = (((0,), (0,)), ((), ()))
OWN = ("x", "y", "c")
CHIPS = ("x", "y")


def spread(block, axes, count):
    copies = jnp.broadcast_to(block[None], (count,) + block.shape)
    return lax.all_to_all(copies, axes, 0, 0, tiled=True)


def per_device(
    inputs, w_gate, w_up, w_down, a_gate, a_up, b_gate, b_up, a_down, b_down, adapter_ids, owner_map
):
    chips = lax.axis_size("x") * lax.axis_size("y")
    cores = lax.axis_size("c")
    parts = lax.axis_size("z")
    owners = chips * cores
    here_owner = lax.axis_index(OWN)
    own_rows, width = inputs.shape
    rows = adapter_ids.shape[0]
    units = w_gate.shape[0]
    rank = a_gate.shape[2]
    rank_part = b_gate.shape[1]
    slots = owner_map.shape[0]

    swap = [(0, 1), (1, 0)]
    half = jnp.broadcast_to(inputs[None], (chips,) + inputs.shape)
    half, a_gate, a_up, b_down = lax.optimization_barrier((half, a_gate, a_up, b_down))
    half = lax.all_to_all(half, CHIPS, 0, 0, tiled=True)
    factors = jnp.concatenate([a_gate[0].T, a_up[0].T, b_down[0]], axis=0)
    other = lax.ppermute(factors, "c", swap)
    shrink_pair = (factors[: 2 * rank], other[: 2 * rank])
    down_pair = jnp.concatenate([factors[2 * rank :], other[2 * rank :]], axis=0)
    half = half.reshape(chips * own_rows, width)

    adapter = adapter_ids[:, 0]
    table = jnp.arange(slots, dtype=jnp.int32)
    row_slot = jnp.sum(jnp.where(adapter[:, None] == table[None, :], owner_map[None, :], 0), axis=1)
    onehot = (row_slot[:, None] == table[None, :]).astype(jnp.int32)
    position = jnp.sum((jnp.cumsum(onehot, axis=0) - onehot) * onehot, axis=1)

    def ordered(values):
        by_core = values.reshape(chips, cores, own_rows).transpose(1, 0, 2)
        by_core = by_core.reshape(cores, chips * own_rows)
        return jnp.where(lax.axis_index("c") == 0, by_core, by_core[::-1]).reshape(rows)

    row_slot, position = ordered(row_slot), ordered(position)
    half_rows = chips * own_rows
    here_core = lax.axis_index("c")
    row_core = jnp.where(jnp.arange(rows) < half_rows, here_core, 1 - here_core)
    worker = row_slot - row_slot % cores + row_core
    apart = (row_slot % cores) ^ row_core
    seat = apart * OCAP + position
    seats = cores * OCAP
    seat_of = jnp.arange(seats, dtype=jnp.int32)
    lane = jnp.arange(LANES, dtype=jnp.int32)
    up_per = LANES // (2 * rank_part)
    up_lines = seats // up_per
    mine = (worker == here_owner)[:half_rows, None] & (seat[:half_rows, None] == seat_of[None, :])
    mine = mine.astype(BF16)
    up_line = worker * up_lines + seat // up_per
    up_lines_all = jnp.arange(owners * up_lines, dtype=jnp.int32)
    up_pick = (up_line[:, None] == up_lines_all[None, :]).astype(BF16)
    up_lane = lane[:, None] // (2 * rank_part) == (seat % up_per)[None, :]
    down_per = LANES // rank_part
    down_lines = seats // down_per
    down_line = worker * down_lines + seat // down_per
    down_lines_all = jnp.arange(owners * down_lines, dtype=jnp.int32)
    down_pick = (down_lines_all[:, None] == down_line[None, :]).astype(BF16)
    down_seat = jnp.arange(down_per, dtype=jnp.int32)[:, None] == (seat % down_per)[None, :]
    down_seat = down_seat.astype(BF16)[:, None, :]
    our_line = down_line[:half_rows, None] - here_owner * down_lines
    ours = (our_line == jnp.arange(down_lines, dtype=jnp.int32)[None, :]).astype(BF16)
    our_seat = (seat % down_per)[:half_rows, None] == (lane // rank_part)[None, :]
    our_slot = jnp.arange(cores * rank, dtype=jnp.int32)[None, :] // rank == apart[:half_rows, None]
    slot_rows = (table[:, None] == row_slot[None, :]).astype(BF16)

    column = jnp.arange(parts * LANES, dtype=jnp.int32)
    gathered = column // LANES * rank_part + column % rank_part
    fold = gathered[:, None] == jnp.arange(cores * rank, dtype=jnp.int32)[None, :] % rank
    masks = (
        slot_rows,
        slot_rows.astype(F32),
        down_pick,
        down_seat,
        ours,
        our_seat,
        our_slot,
        up_pick,
        fold.astype(BF16),
        shrink_pair,
    )
    half, masks = lax.optimization_barrier((half, masks))
    slot_rows, slot_mask, down_pick, down_seat, ours, our_seat, our_slot, up_pick = masks[:8]
    fold, shrink_pair = masks[8:]
    selected = lax.dot_general(mine, half, TN, preferred_element_type=F32).astype(BF16)
    shrunk = jnp.concatenate(
        [
            lax.dot_general(
                selected[u * OCAP : (u + 1) * OCAP],
                shrink_pair[u],
                NT,
                preferred_element_type=F32,
            )
            for u in range(cores)
        ],
        axis=0,
    ).astype(BF16)
    part, seat_up = column // LANES, column % LANES // (2 * rank_part)
    low = column % (2 * rank_part)
    source = part * rank_part + low % rank_part + low // rank_part * rank
    move = (jnp.arange(2 * rank, dtype=jnp.int32)[:, None] == source[None, :]).astype(BF16)
    shrunk = jnp.dot(shrunk, move, preferred_element_type=F32)
    shrunk = jnp.where(seat_of[:, None] % up_per == seat_up[None, :], shrunk, 0).astype(BF16)
    line_of = jnp.arange(up_lines, dtype=jnp.int32)[:, None] == seat_of[None, :] // up_per
    shrunk = jnp.dot(line_of.astype(BF16), shrunk, preferred_element_type=F32).astype(BF16)
    shrunk = shrunk.reshape(up_lines, parts, LANES).transpose(1, 0, 2)
    shrunk = lax.all_to_all(shrunk, "z", 0, 0, tiled=True)
    half, shrunk = lax.optimization_barrier((half, shrunk))
    piece = jnp.concatenate([half, lax.ppermute(half, "c", swap)], axis=0)
    shrunk = jnp.sum(shrunk.astype(F32), axis=0).astype(BF16)
    low_all = spread(shrunk, OWN, owners)
    gate_base = lax.dot_general(w_gate, piece, NT, preferred_element_type=F32)
    up_base = lax.dot_general(w_up, piece, NT, preferred_element_type=F32)
    low_all, gate_base, up_base = lax.optimization_barrier((low_all, gate_base, up_base))
    low_rows = lax.dot_general(
        low_all.reshape(owners * up_lines, LANES),
        up_pick,
        (((0,), (1,)), ((), ())),
        preferred_element_type=F32,
    )
    low_rows = jnp.where(up_lane, low_rows, 0).astype(BF16)
    gather_up = jnp.arange(2 * rank_part, dtype=jnp.int32)[:, None] == lane[None, :] % (2 * rank_part)
    low_rows = jnp.dot(gather_up.astype(BF16), low_rows, preferred_element_type=F32).astype(BF16)

    def expand(low, weights):
        wide = (slot_rows[:, None, :] * low[None, :, :]).reshape(slots * rank_part, rows)
        return lax.dot_general(
            weights.reshape(slots * rank_part, units), wide, TN, preferred_element_type=F32
        )

    gate_part = gate_base + expand(low_rows[:rank_part], b_gate)
    up_part = up_base + expand(low_rows[rank_part:], b_up)
    both = jnp.stack(
        [
            gate_part.astype(BF16).reshape(parts, units // parts, rows),
            up_part.astype(BF16).reshape(parts, units // parts, rows),
        ],
        axis=1,
    )
    both = lax.all_to_all(both, "z", 0, 0, tiled=True)
    both = jnp.sum(both.astype(F32), axis=0)
    hidden = (jax.nn.silu(both[0]) * both[1]).astype(BF16)
    hidden_all = spread(hidden, "z", parts).reshape(units, rows)

    rank_full = lax.dot_general(
        a_down.reshape(units, slots * rank_part), hidden_all, TN, preferred_element_type=F32
    )
    rank_rows = jnp.sum(
        rank_full.reshape(slots, rank_part, rows) * slot_mask[:, None, :], axis=0
    ).astype(BF16)
    rank_wide = (down_seat * rank_rows[None, :, :]).reshape(LANES, rows)
    rank_sent = lax.dot_general(down_pick, rank_wide, NT, preferred_element_type=F32).astype(BF16)
    rank_sum = lax.all_to_all(
        rank_sent.reshape(owners, down_lines, LANES), OWN, 0, 0, tiled=True
    )
    out = lax.dot_general(hidden_all, w_down, TN, preferred_element_type=F32)
    kept, given = out[:half_rows], out[half_rows:].astype(BF16)
    rank_sum, kept, given = lax.optimization_barrier((rank_sum, kept, given))
    rank_sum = jnp.sum(rank_sum.astype(F32), axis=0).astype(BF16)
    rank_all = spread(rank_sum, "z", parts)
    out = kept + lax.ppermute(given, "c", swap).astype(F32)
    rank_ours = lax.dot_general(
        ours, rank_all, (((1,), (1,)), ((), ())), preferred_element_type=F32
    )
    rank_ours = jnp.where(our_seat[:, None, :], rank_ours, 0).astype(BF16)
    rank_ours = jnp.dot(
        rank_ours.reshape(half_rows, parts * LANES),
        fold,
        preferred_element_type=F32,
    )
    rank_ours = jnp.where(our_slot, rank_ours, 0).astype(BF16)
    out = out + jnp.dot(rank_ours, down_pair, preferred_element_type=F32)
    out = out.astype(BF16)
    out = lax.all_to_all(out.reshape(chips, own_rows, width), CHIPS, 0, 0, tiled=True)
    return jnp.sum(out.astype(F32), axis=0).astype(BF16)


def solution(mesh):
    side = (4, 8, 2, 8)
    fine = Mesh(mesh.devices.reshape(side), ("x", "y", "c", "z"))
    ad, tp = ("x", "y", "c"), "z"
    placed = (
        P(ad, tp),
        P(ad, tp),
        P(ad, tp),
        P(ad, tp),
        P(ad, tp, None),
        P(ad, tp, None),
        P(None, tp, ad),
        P(None, tp, ad),
        P(ad, None, tp),
        P(ad, None, tp),
        P(),
        P(),
    )
    return jax.shard_map(
        per_device, mesh=fine, in_specs=placed, out_specs=P(ad, tp), check_vma=False
    )
```

```python
import jax
import jax.numpy as jnp
from jax import lax
from jax.sharding import Mesh, PartitionSpec as P

OCAP = 24
LANES = 128
F32 = jnp.float32
BF16 = jnp.bfloat16
NT = (((1,), (1,)), ((), ()))
TN = (((0,), (0,)), ((), ()))
OWN = ("x", "y", "c")
CHIPS = ("x", "y")


def spread(block, axes, count):
    copies = jnp.broadcast_to(block[None], (count,) + block.shape)
    return lax.all_to_all(copies, axes, 0, 0, tiled=True)


def per_device(
    inputs, w_gate, w_up, w_down, a_gate, a_up, b_gate, b_up, a_down, b_down, adapter_ids, owner_map
):
    chips = lax.axis_size("x") * lax.axis_size("y")
    cores = lax.axis_size("c")
    parts = lax.axis_size("z")
    owners = chips * cores
    here_owner = lax.axis_index(OWN)
    own_rows, width = inputs.shape
    rows = adapter_ids.shape[0]
    units = w_gate.shape[0]
    rank = a_gate.shape[2]
    rank_part = b_gate.shape[1]
    slots = owner_map.shape[0]

    swap = [(0, 1), (1, 0)]
    half = jnp.broadcast_to(inputs[None], (chips,) + inputs.shape)
    half, a_gate, a_up, b_down = lax.optimization_barrier((half, a_gate, a_up, b_down))
    half = lax.all_to_all(half, CHIPS, 0, 0, tiled=True)
    factors = jnp.concatenate([a_gate[0].T, a_up[0].T, b_down[0]], axis=0)
    other = lax.ppermute(factors, "c", swap)
    shrink_pair = (factors[: 2 * rank], other[: 2 * rank])
    down_pair = jnp.concatenate([factors[2 * rank :], other[2 * rank :]], axis=0)
    half = half.reshape(chips * own_rows, width)

    adapter = adapter_ids[:, 0]
    table = jnp.arange(slots, dtype=jnp.int32)
    row_slot = jnp.sum(jnp.where(adapter[:, None] == table[None, :], owner_map[None, :], 0), axis=1)
    onehot = (row_slot[:, None] == table[None, :]).astype(jnp.int32)
    position = jnp.sum((jnp.cumsum(onehot, axis=0) - onehot) * onehot, axis=1)

    def ordered(values):
        by_core = values.reshape(chips, cores, own_rows).transpose(1, 0, 2)
        by_core = by_core.reshape(cores, chips * own_rows)
        return jnp.where(lax.axis_index("c") == 0, by_core, by_core[::-1]).reshape(rows)

    row_slot, position = ordered(row_slot), ordered(position)
    half_rows = chips * own_rows
    here_core = lax.axis_index("c")
    row_core = jnp.where(jnp.arange(rows) < half_rows, here_core, 1 - here_core)
    worker = row_slot - row_slot % cores + row_core
    apart = (row_slot % cores) ^ row_core
    seat = apart * OCAP + position
    seats = cores * OCAP
    seat_of = jnp.arange(seats, dtype=jnp.int32)
    lane = jnp.arange(LANES, dtype=jnp.int32)
    up_per = LANES // (2 * rank_part)
    up_lines = seats // up_per
    mine = (worker == here_owner)[:half_rows, None] & (seat[:half_rows, None] == seat_of[None, :])
    mine = mine.astype(BF16)
    up_line = worker * up_lines + seat // up_per
    up_lines_all = jnp.arange(owners * up_lines, dtype=jnp.int32)
    up_pick = (up_line[:, None] == up_lines_all[None, :]).astype(BF16)
    up_lane = lane[:, None] // (2 * rank_part) == (seat % up_per)[None, :]
    down_per = LANES // rank_part
    down_lines = seats // down_per
    down_line = worker * down_lines + seat // down_per
    down_lines_all = jnp.arange(owners * down_lines, dtype=jnp.int32)
    down_pick = (down_lines_all[:, None] == down_line[None, :]).astype(BF16)
    down_seat = jnp.arange(down_per, dtype=jnp.int32)[:, None] == (seat % down_per)[None, :]
    down_seat = down_seat.astype(BF16)[:, None, :]
    our_line = down_line[:half_rows, None] - here_owner * down_lines
    ours = (our_line == jnp.arange(down_lines, dtype=jnp.int32)[None, :]).astype(BF16)
    our_seat = (seat % down_per)[:half_rows, None] == (lane // rank_part)[None, :]
    our_slot = jnp.arange(cores * rank, dtype=jnp.int32)[None, :] // rank == apart[:half_rows, None]
    slot_rows = (table[:, None] == row_slot[None, :]).astype(BF16)

    column = jnp.arange(parts * LANES, dtype=jnp.int32)
    gathered = column // LANES * rank_part + column % rank_part
    fold = gathered[:, None] == jnp.arange(cores * rank, dtype=jnp.int32)[None, :] % rank
    gather_up = jnp.arange(2 * rank_part, dtype=jnp.int32)[:, None] == lane[None, :] % (2 * rank_part)
    masks = (
        (slot_rows[:, :half_rows], slot_rows[:, half_rows:]),
        slot_rows.astype(F32),
        down_pick,
        down_seat,
        ours,
        our_seat,
        our_slot,
        (up_pick, up_lane, gather_up.astype(BF16)),
        fold.astype(BF16),
        shrink_pair,
        jnp.stack([b_gate.reshape(slots * rank_part, units), b_up.reshape(slots * rank_part, units)]),
    )
    half, masks = lax.optimization_barrier((half, masks))
    slot_halves, slot_mask, down_pick, down_seat, ours, our_seat, our_slot, ups = masks[:8]
    up_pick, up_lane, gather_up = ups
    fold, shrink_pair, expand_pair = masks[8:]
    selected = lax.dot_general(mine, half, TN, preferred_element_type=F32).astype(BF16)
    shrunk = jnp.concatenate(
        [
            lax.dot_general(
                selected[u * OCAP : (u + 1) * OCAP],
                shrink_pair[u],
                NT,
                preferred_element_type=F32,
            )
            for u in range(cores)
        ],
        axis=0,
    ).astype(BF16)
    part, seat_up = column // LANES, column % LANES // (2 * rank_part)
    low = column % (2 * rank_part)
    source = part * rank_part + low % rank_part + low // rank_part * rank
    move = (jnp.arange(2 * rank, dtype=jnp.int32)[:, None] == source[None, :]).astype(BF16)
    shrunk = jnp.dot(shrunk, move, preferred_element_type=F32)
    shrunk = jnp.where(seat_of[:, None] % up_per == seat_up[None, :], shrunk, 0).astype(BF16)
    line_of = jnp.arange(up_lines, dtype=jnp.int32)[:, None] == seat_of[None, :] // up_per
    shrunk = jnp.dot(line_of.astype(BF16), shrunk, preferred_element_type=F32).astype(BF16)
    shrunk = shrunk.reshape(up_lines, parts, LANES).transpose(1, 0, 2)
    shrunk = lax.all_to_all(shrunk, "z", 0, 0, tiled=True)
    shrunk = jnp.sum(shrunk.astype(F32), axis=0).astype(BF16)
    shrunk = jnp.broadcast_to(shrunk[None], (owners,) + shrunk.shape)
    half, shrunk = lax.optimization_barrier((half, shrunk))
    low_all = lax.all_to_all(shrunk, OWN, 0, 0, tiled=True)
    far = lax.ppermute(half, "c", swap)
    base = [lax.dot_general(w, half, NT, preferred_element_type=F32) for w in (w_gate, w_up)]
    low_all, base = lax.optimization_barrier((low_all, base))
    far_base = [lax.dot_general(w, far, NT, preferred_element_type=F32) for w in (w_gate, w_up)]
    low_rows = lax.dot_general(
        low_all.reshape(owners * up_lines, LANES),
        up_pick,
        (((0,), (1,)), ((), ())),
        preferred_element_type=F32,
    )
    low_rows = jnp.where(up_lane, low_rows, 0).astype(BF16)
    low_rows = jnp.dot(gather_up, low_rows, preferred_element_type=F32).astype(BF16)

    def expand(low, weights, hot):
        wide = (hot[:, None, :] * low[None, :, :]).reshape(slots * rank_part, half_rows)
        return lax.dot_general(weights, wide, TN, preferred_element_type=F32)

    def by_part(terms, cols):
        low = low_rows[:, cols * half_rows : (cols + 1) * half_rows]
        low = (low[:rank_part], low[rank_part:])
        hot = slot_halves[cols]
        sums = [terms[i] + expand(low[i], expand_pair[i], hot) for i in range(2)]
        sums = [v.astype(BF16).reshape(parts, units // parts, half_rows) for v in sums]
        return jnp.stack(sums, axis=1)

    both = jnp.concatenate(
        [by_part(base, 0), by_part(far_base, 1)],
        axis=3,
    )
    both = lax.all_to_all(both, "z", 0, 0, tiled=True)
    both = jnp.sum(both.astype(F32), axis=0)
    hidden = (jax.nn.silu(both[0]) * both[1]).astype(BF16)
    hidden_all = spread(hidden, "z", parts).reshape(units, rows)

    rank_full = lax.dot_general(
        a_down.reshape(units, slots * rank_part), hidden_all, TN, preferred_element_type=F32
    )
    rank_rows = jnp.sum(
        rank_full.reshape(slots, rank_part, rows) * slot_mask[:, None, :], axis=0
    ).astype(BF16)
    rank_wide = (down_seat * rank_rows[None, :, :]).reshape(LANES, rows)
    rank_sent = lax.dot_general(down_pick, rank_wide, NT, preferred_element_type=F32).astype(BF16)
    rank_sum = lax.all_to_all(
        rank_sent.reshape(owners, down_lines, LANES), OWN, 0, 0, tiled=True
    )
    out = lax.dot_general(hidden_all, w_down, TN, preferred_element_type=F32)
    kept, given = out[:half_rows], out[half_rows:].astype(BF16)
    rank_sum, kept, given = lax.optimization_barrier((rank_sum, kept, given))
    rank_sum = jnp.sum(rank_sum.astype(F32), axis=0).astype(BF16)
    rank_all = spread(rank_sum, "z", parts)
    out = kept + lax.ppermute(given, "c", swap).astype(F32)
    rank_ours = lax.dot_general(
        ours, rank_all, (((1,), (1,)), ((), ())), preferred_element_type=F32
    )
    rank_ours = jnp.where(our_seat[:, None, :], rank_ours, 0).astype(BF16)
    rank_ours = jnp.dot(
        rank_ours.reshape(half_rows, parts * LANES),
        fold,
        preferred_element_type=F32,
    )
    rank_ours = jnp.where(our_slot, rank_ours, 0).astype(BF16)
    out = out + jnp.dot(rank_ours, down_pair, preferred_element_type=F32)
    out = out.astype(BF16)
    out = lax.all_to_all(out.reshape(chips, own_rows, width), CHIPS, 0, 0, tiled=True)
    return jnp.sum(out.astype(F32), axis=0).astype(BF16)


def solution(mesh):
    side = (4, 8, 2, 8)
    fine = Mesh(mesh.devices.reshape(side), ("x", "y", "c", "z"))
    ad, tp = ("x", "y", "c"), "z"
    placed = (
        P(ad, tp),
        P(ad, tp),
        P(ad, tp),
        P(ad, tp),
        P(ad, tp, None),
        P(ad, tp, None),
        P(None, tp, ad),
        P(None, tp, ad),
        P(ad, None, tp),
        P(ad, None, tp),
        P(),
        P(),
    )
    return jax.shard_map(
        per_device, mesh=fine, in_specs=placed, out_specs=P(ad, tp), check_vma=False
    )
```

```python
import jax
import jax.numpy as jnp
from jax import lax
from jax.sharding import Mesh, PartitionSpec as P

OCAP = 24
LANES = 128
F32 = jnp.float32
BF16 = jnp.bfloat16
NT = (((1,), (1,)), ((), ()))
TN = (((0,), (0,)), ((), ()))
OWN = ("x", "y", "c")
CHIPS = ("x", "y")


def spread(block, axes, count):
    copies = jnp.broadcast_to(block[None], (count,) + block.shape)
    return lax.all_to_all(copies, axes, 0, 0, tiled=True)


def per_device(
    inputs, w_gate, w_up, w_down, a_gate, a_up, b_gate, b_up, a_down, b_down, adapter_ids, owner_map
):
    chips = lax.axis_size("x") * lax.axis_size("y")
    cores = lax.axis_size("c")
    parts = lax.axis_size("z")
    owners = chips * cores
    here_owner = lax.axis_index(OWN)
    own_rows, width = inputs.shape
    rows = adapter_ids.shape[0]
    units = w_gate.shape[0]
    rank = a_gate.shape[2]
    rank_part = b_gate.shape[1]
    slots = owner_map.shape[0]

    swap = [(0, 1), (1, 0)]
    half = jnp.broadcast_to(inputs[None], (chips,) + inputs.shape)
    half, a_gate, a_up, b_down = lax.optimization_barrier((half, a_gate, a_up, b_down))
    half = lax.all_to_all(half, CHIPS, 0, 0, tiled=True)
    factors = jnp.concatenate([a_gate[0].T, a_up[0].T, b_down[0]], axis=0)
    other = lax.ppermute(factors, "c", swap)
    shrink_pair = (factors[: 2 * rank], other[: 2 * rank])
    down_pair = jnp.concatenate([factors[2 * rank :], other[2 * rank :]], axis=0)
    half = half.reshape(chips * own_rows, width)

    adapter = adapter_ids[:, 0]
    table = jnp.arange(slots, dtype=jnp.int32)
    row_slot = jnp.sum(jnp.where(adapter[:, None] == table[None, :], owner_map[None, :], 0), axis=1)
    onehot = (row_slot[:, None] == table[None, :]).astype(jnp.int32)
    position = jnp.sum((jnp.cumsum(onehot, axis=0) - onehot) * onehot, axis=1)

    def ordered(values):
        by_core = values.reshape(chips, cores, own_rows).transpose(1, 0, 2)
        by_core = by_core.reshape(cores, chips * own_rows)
        return jnp.where(lax.axis_index("c") == 0, by_core, by_core[::-1]).reshape(rows)

    row_slot, position = ordered(row_slot), ordered(position)
    half_rows = chips * own_rows
    here_core = lax.axis_index("c")
    row_core = jnp.where(jnp.arange(rows) < half_rows, here_core, 1 - here_core)
    worker = row_slot - row_slot % cores + row_core
    apart = (row_slot % cores) ^ row_core
    seat = apart * OCAP + position
    seats = cores * OCAP
    seat_of = jnp.arange(seats, dtype=jnp.int32)
    lane = jnp.arange(LANES, dtype=jnp.int32)
    up_per = LANES // (2 * rank_part)
    up_lines = seats // up_per
    mine = (worker == here_owner)[:half_rows, None] & (seat[:half_rows, None] == seat_of[None, :])
    mine = mine.astype(BF16)
    up_line = worker * up_lines + seat // up_per
    up_lines_all = jnp.arange(owners * up_lines, dtype=jnp.int32)
    up_pick = (up_line[:, None] == up_lines_all[None, :]).astype(BF16)
    up_lane = lane[:, None] // (2 * rank_part) == (seat % up_per)[None, :]
    down_per = LANES // rank_part
    down_lines = seats // down_per
    down_line = worker * down_lines + seat // down_per
    down_lines_all = jnp.arange(owners * down_lines, dtype=jnp.int32)
    down_pick = (down_lines_all[:, None] == down_line[None, :]).astype(BF16)
    down_seat = jnp.arange(down_per, dtype=jnp.int32)[:, None] == (seat % down_per)[None, :]
    down_seat = down_seat.astype(BF16)[:, None, :]
    our_line = down_line[:half_rows, None] - here_owner * down_lines
    ours = (our_line == jnp.arange(down_lines, dtype=jnp.int32)[None, :]).astype(BF16)
    our_seat = (seat % down_per)[:half_rows, None] == (lane // rank_part)[None, :]
    our_slot = jnp.arange(cores * rank, dtype=jnp.int32)[None, :] // rank == apart[:half_rows, None]
    slot_rows = (table[:, None] == row_slot[None, :]).astype(BF16)

    column = jnp.arange(parts * LANES, dtype=jnp.int32)
    gathered = column // LANES * rank_part + column % rank_part
    fold = gathered[:, None] == jnp.arange(cores * rank, dtype=jnp.int32)[None, :] % rank
    one = lax.optimization_barrier(jnp.ones((), BF16))
    masks = (
        slot_rows,
        slot_rows.astype(F32),
        down_pick,
        down_seat,
        ours,
        our_seat.astype(BF16),
        our_slot.astype(BF16),
        up_pick,
        fold.astype(BF16),
        shrink_pair,
        b_gate * one,
    )
    half, masks = lax.optimization_barrier((half, masks))
    slot_rows, slot_mask, down_pick, down_seat, ours, our_seat, our_slot, up_pick = masks[:8]
    fold, shrink_pair, b_gate = masks[8:]
    selected = lax.dot_general(mine, half, TN, preferred_element_type=F32).astype(BF16)
    shrunk = jnp.concatenate(
        [
            lax.dot_general(
                selected[u * OCAP : (u + 1) * OCAP],
                shrink_pair[u],
                NT,
                preferred_element_type=F32,
            )
            for u in range(cores)
        ],
        axis=0,
    ).astype(BF16)
    part, seat_up = column // LANES, column % LANES // (2 * rank_part)
    low = column % (2 * rank_part)
    source = part * rank_part + low % rank_part + low // rank_part * rank
    move = (jnp.arange(2 * rank, dtype=jnp.int32)[:, None] == source[None, :]).astype(BF16)
    shrunk = jnp.dot(shrunk, move, preferred_element_type=F32)
    shrunk = jnp.where(seat_of[:, None] % up_per == seat_up[None, :], shrunk, 0).astype(BF16)
    line_of = jnp.arange(up_lines, dtype=jnp.int32)[:, None] == seat_of[None, :] // up_per
    shrunk = jnp.dot(line_of.astype(BF16), shrunk, preferred_element_type=F32).astype(BF16)
    shrunk = shrunk.reshape(up_lines, parts, LANES).transpose(1, 0, 2)
    shrunk = lax.all_to_all(shrunk, "z", 0, 0, tiled=True)
    half, shrunk = lax.optimization_barrier((half, shrunk))
    piece = jnp.concatenate([half, lax.ppermute(half, "c", swap)], axis=0)
    shrunk = jnp.sum(shrunk.astype(F32), axis=0).astype(BF16)
    low_all = spread(shrunk, OWN, owners)
    gate_base = lax.dot_general(w_gate, piece, NT, preferred_element_type=F32)
    up_base = lax.dot_general(w_up, piece, NT, preferred_element_type=F32)
    low_all, gate_base, up_base = lax.optimization_barrier((low_all, gate_base, up_base))
    low_rows = lax.dot_general(
        low_all.reshape(owners * up_lines, LANES),
        up_pick,
        (((0,), (1,)), ((), ())),
        preferred_element_type=F32,
    )
    low_rows = jnp.where(up_lane, low_rows, 0).astype(BF16)
    gather_up = jnp.arange(2 * rank_part, dtype=jnp.int32)[:, None] == lane[None, :] % (2 * rank_part)
    low_rows = jnp.dot(gather_up.astype(BF16), low_rows, preferred_element_type=F32).astype(BF16)

    def expand(low, weights):
        wide = (slot_rows[:, None, :] * low[None, :, :]).reshape(slots * rank_part, rows)
        return lax.dot_general(
            weights.reshape(slots * rank_part, units), wide, TN, preferred_element_type=F32
        )

    gate_part = gate_base + expand(low_rows[:rank_part], b_gate)
    up_part = up_base + expand(low_rows[rank_part:], b_up)
    both = jnp.stack(
        [
            gate_part.astype(BF16).reshape(parts, units // parts, rows),
            up_part.astype(BF16).reshape(parts, units // parts, rows),
        ],
        axis=1,
    )
    both = lax.all_to_all(both, "z", 0, 0, tiled=True)
    both = jnp.sum(both.astype(F32), axis=0)
    hidden = (jax.nn.silu(both[0]) * both[1]).astype(BF16)
    hidden_all = spread(hidden, "z", parts).reshape(units, rows)

    rank_full = lax.dot_general(
        a_down.reshape(units, slots * rank_part), hidden_all, TN, preferred_element_type=F32
    )
    rank_rows = jnp.sum(
        rank_full.reshape(slots, rank_part, rows) * slot_mask[:, None, :], axis=0
    ).astype(BF16)
    rank_wide = (down_seat * rank_rows[None, :, :]).reshape(LANES, rows)
    rank_sent = lax.dot_general(down_pick, rank_wide, NT, preferred_element_type=F32).astype(BF16)
    rank_sum = lax.all_to_all(
        rank_sent.reshape(owners, down_lines, LANES), OWN, 0, 0, tiled=True
    )
    out = lax.dot_general(hidden_all, w_down, TN, preferred_element_type=F32)
    kept, given = out[:half_rows], out[half_rows:].astype(BF16)
    rank_sum, kept, given = lax.optimization_barrier((rank_sum, kept, given))
    rank_sum = jnp.sum(rank_sum.astype(F32), axis=0).astype(BF16)
    rank_all = spread(rank_sum, "z", parts)
    out = kept + lax.ppermute(given, "c", swap).astype(F32)
    rank_ours = lax.dot_general(
        ours, rank_all, (((1,), (1,)), ((), ())), preferred_element_type=F32
    )
    rank_ours = rank_ours.astype(BF16) * our_seat[:, None, :]
    rank_ours = jnp.dot(
        rank_ours.reshape(half_rows, parts * LANES),
        fold,
        preferred_element_type=F32,
    )
    rank_ours = rank_ours.astype(BF16) * our_slot
    out = out + jnp.dot(rank_ours, down_pair, preferred_element_type=F32)
    out = out.astype(BF16)
    out = lax.all_to_all(out.reshape(chips, own_rows, width), CHIPS, 0, 0, tiled=True)
    return jnp.sum(out.astype(F32), axis=0).astype(BF16)


def solution(mesh):
    side = (4, 8, 2, 8)
    fine = Mesh(mesh.devices.reshape(side), ("x", "y", "c", "z"))
    ad, tp = ("x", "y", "c"), "z"
    placed = (
        P(ad, tp),
        P(ad, tp),
        P(ad, tp),
        P(ad, tp),
        P(ad, tp, None),
        P(ad, tp, None),
        P(None, tp, ad),
        P(None, tp, ad),
        P(ad, None, tp),
        P(ad, None, tp),
        P(),
        P(),
    )
    return jax.shard_map(
        per_device, mesh=fine, in_specs=placed, out_specs=P(ad, tp), check_vma=False
    )
```

```python
import jax
import jax.numpy as jnp
from jax import lax
from jax.sharding import Mesh, PartitionSpec as P

OCAP = 24
LANES = 128
F32 = jnp.float32
BF16 = jnp.bfloat16
NT = (((1,), (1,)), ((), ()))
TN = (((0,), (0,)), ((), ()))
OWN = ("x", "y", "c")
CHIPS = ("x", "y")


def spread(block, axes, count):
    copies = jnp.broadcast_to(block[None], (count,) + block.shape)
    return lax.all_to_all(copies, axes, 0, 0, tiled=True)


def per_device(
    inputs, w_gate, w_up, w_down, a_gate, a_up, b_gate, b_up, a_down, b_down, adapter_ids, owner_map
):
    chips = lax.axis_size("x") * lax.axis_size("y")
    cores = lax.axis_size("c")
    parts = lax.axis_size("z")
    owners = chips * cores
    here_owner = lax.axis_index(OWN)
    own_rows, width = inputs.shape
    rows = adapter_ids.shape[0]
    units = w_gate.shape[0]
    rank = a_gate.shape[2]
    rank_part = b_gate.shape[1]
    slots = owner_map.shape[0]

    swap = [(0, 1), (1, 0)]
    half = jnp.broadcast_to(inputs[None], (chips,) + inputs.shape)
    half, a_gate, a_up, b_down = lax.optimization_barrier((half, a_gate, a_up, b_down))
    half = lax.all_to_all(half, CHIPS, 0, 0, tiled=True)
    factors = jnp.concatenate([a_gate[0].T, a_up[0].T, b_down[0]], axis=0)
    other = lax.ppermute(factors, "c", swap)
    shrink_pair = (factors[: 2 * rank], other[: 2 * rank])
    down_pair = jnp.concatenate([factors[2 * rank :], other[2 * rank :]], axis=0)
    half = half.reshape(chips * own_rows, width)

    adapter = adapter_ids[:, 0]
    table = jnp.arange(slots, dtype=jnp.int32)
    row_slot = jnp.sum(jnp.where(adapter[:, None] == table[None, :], owner_map[None, :], 0), axis=1)
    onehot = (row_slot[:, None] == table[None, :]).astype(jnp.int32)
    position = jnp.sum((jnp.cumsum(onehot, axis=0) - onehot) * onehot, axis=1)

    def ordered(values):
        by_core = values.reshape(chips, cores, own_rows).transpose(1, 0, 2)
        by_core = by_core.reshape(cores, chips * own_rows)
        return jnp.where(lax.axis_index("c") == 0, by_core, by_core[::-1]).reshape(rows)

    row_slot, position = ordered(row_slot), ordered(position)
    half_rows = chips * own_rows
    here_core = lax.axis_index("c")
    row_core = jnp.where(jnp.arange(rows) < half_rows, here_core, 1 - here_core)
    worker = row_slot - row_slot % cores + row_core
    apart = (row_slot % cores) ^ row_core
    seat = apart * OCAP + position
    seats = cores * OCAP
    seat_of = jnp.arange(seats, dtype=jnp.int32)
    lane = jnp.arange(LANES, dtype=jnp.int32)
    up_per = LANES // (2 * rank_part)
    up_lines = seats // up_per
    mine = (worker == here_owner)[:half_rows, None] & (seat[:half_rows, None] == seat_of[None, :])
    mine = mine.astype(BF16)
    up_line = worker * up_lines + seat // up_per
    up_lines_all = jnp.arange(owners * up_lines, dtype=jnp.int32)
    up_pick = (up_line[:, None] == up_lines_all[None, :]).astype(BF16)
    up_lane = lane[:, None] // (2 * rank_part) == (seat % up_per)[None, :]
    down_per = LANES // rank_part
    down_lines = seats // down_per
    down_line = worker * down_lines + seat // down_per
    down_lines_all = jnp.arange(owners * down_lines, dtype=jnp.int32)
    down_pick = (down_lines_all[:, None] == down_line[None, :]).astype(BF16)
    down_seat = jnp.arange(down_per, dtype=jnp.int32)[:, None] == (seat % down_per)[None, :]
    down_seat = down_seat.astype(BF16)[:, None, :]
    our_line = down_line[:half_rows, None] - here_owner * down_lines
    ours = (our_line == jnp.arange(down_lines, dtype=jnp.int32)[None, :]).astype(BF16)
    our_seat = (seat % down_per)[:half_rows, None] == (lane // rank_part)[None, :]
    our_slot = jnp.arange(cores * rank, dtype=jnp.int32)[None, :] // rank == apart[:half_rows, None]
    slot_rows = (table[:, None] == row_slot[None, :]).astype(BF16)

    column = jnp.arange(parts * LANES, dtype=jnp.int32)
    gathered = column // LANES * rank_part + column % rank_part
    fold = gathered[:, None] == jnp.arange(cores * rank, dtype=jnp.int32)[None, :] % rank
    one = lax.optimization_barrier(jnp.ones((), BF16))
    masks = (
        slot_rows.astype(F32),
        down_pick,
        down_seat,
        ours,
        our_seat,
        our_slot,
        fold.astype(BF16),
        shrink_pair,
        b_gate * one,
    )
    half, masks = lax.optimization_barrier((half, masks))
    slot_mask, down_pick, down_seat, ours, our_seat, our_slot = masks[:6]
    fold, shrink_pair, b_gate = masks[6:]
    selected = lax.dot_general(mine, half, TN, preferred_element_type=F32).astype(BF16)
    shrunk = jnp.concatenate(
        [
            lax.dot_general(
                selected[u * OCAP : (u + 1) * OCAP],
                shrink_pair[u],
                NT,
                preferred_element_type=F32,
            )
            for u in range(cores)
        ],
        axis=0,
    ).astype(BF16)
    part, seat_up = column // LANES, column % LANES // (2 * rank_part)
    low = column % (2 * rank_part)
    source = part * rank_part + low % rank_part + low // rank_part * rank
    move = (jnp.arange(2 * rank, dtype=jnp.int32)[:, None] == source[None, :]).astype(BF16)
    shrunk = jnp.dot(shrunk, move, preferred_element_type=F32)
    shrunk = jnp.where(seat_of[:, None] % up_per == seat_up[None, :], shrunk, 0).astype(BF16)
    line_of = jnp.arange(up_lines, dtype=jnp.int32)[:, None] == seat_of[None, :] // up_per
    shrunk = jnp.dot(line_of.astype(BF16), shrunk, preferred_element_type=F32).astype(BF16)
    shrunk = shrunk.reshape(up_lines, parts, LANES).transpose(1, 0, 2)
    shrunk = lax.all_to_all(shrunk, "z", 0, 0, tiled=True)
    half, shrunk = lax.optimization_barrier((half, shrunk))
    piece = jnp.concatenate([half, lax.ppermute(half, "c", swap)], axis=0)
    shrunk = jnp.sum(shrunk.astype(F32), axis=0).astype(BF16)
    low_all = spread(shrunk, OWN, owners)
    gate_base = lax.dot_general(w_gate, piece, NT, preferred_element_type=F32)
    up_base = lax.dot_general(w_up, piece, NT, preferred_element_type=F32)
    low_all, gate_base, up_base = lax.optimization_barrier((low_all, gate_base, up_base))
    low_rows = lax.dot_general(
        low_all.reshape(owners * up_lines, LANES),
        up_pick,
        (((0,), (1,)), ((), ())),
        preferred_element_type=F32,
    )
    low_rows = jnp.where(up_lane, low_rows, 0).astype(BF16)
    gather_up = jnp.arange(2 * rank_part, dtype=jnp.int32)[:, None] == lane[None, :] % (2 * rank_part)
    low_rows = jnp.dot(gather_up.astype(BF16), low_rows, preferred_element_type=F32).astype(BF16)

    def expand(low, weights):
        wide = (slot_mask.astype(BF16)[:, None, :] * low[None, :, :]).reshape(slots * rank_part, rows)
        return lax.dot_general(
            weights.reshape(slots * rank_part, units), wide, TN, preferred_element_type=F32
        )

    gate_part = gate_base + expand(low_rows[:rank_part], b_gate)
    up_part = up_base + expand(low_rows[rank_part:], b_up)
    both = jnp.stack(
        [
            gate_part.astype(BF16).reshape(parts, units // parts, rows),
            up_part.astype(BF16).reshape(parts, units // parts, rows),
        ],
        axis=1,
    )
    both = lax.all_to_all(both, "z", 0, 0, tiled=True)
    both = jnp.sum(both.astype(F32), axis=0)
    hidden = (jax.nn.silu(both[0]) * both[1]).astype(BF16)
    hidden_all = spread(hidden, "z", parts).reshape(units, rows)

    rank_full = lax.dot_general(
        a_down.reshape(units, slots * rank_part), hidden_all, TN, preferred_element_type=F32
    )
    rank_rows = jnp.sum(
        rank_full.reshape(slots, rank_part, rows) * slot_mask[:, None, :], axis=0
    ).astype(BF16)
    rank_wide = (down_seat * rank_rows[None, :, :]).reshape(LANES, rows)
    rank_sent = lax.dot_general(down_pick, rank_wide, NT, preferred_element_type=F32).astype(BF16)
    rank_sum = lax.all_to_all(
        rank_sent.reshape(owners, down_lines, LANES), OWN, 0, 0, tiled=True
    )
    out = lax.dot_general(hidden_all, w_down, TN, preferred_element_type=F32)
    kept, given = out[:half_rows], out[half_rows:].astype(BF16)
    rank_sum, kept, given = lax.optimization_barrier((rank_sum, kept, given))
    rank_sum = jnp.sum(rank_sum.astype(F32), axis=0).astype(BF16)
    rank_all = spread(rank_sum, "z", parts)
    out = kept + lax.ppermute(given, "c", swap).astype(F32)
    rank_ours = lax.dot_general(
        ours, rank_all, (((1,), (1,)), ((), ())), preferred_element_type=F32
    )
    rank_ours = jnp.where(our_seat[:, None, :], rank_ours, 0).astype(BF16)
    rank_ours = jnp.dot(
        rank_ours.reshape(half_rows, parts * LANES),
        fold,
        preferred_element_type=F32,
    )
    rank_ours = jnp.where(our_slot, rank_ours, 0).astype(BF16)
    out = out + jnp.dot(rank_ours, down_pair, preferred_element_type=F32)
    out = out.astype(BF16)
    out = lax.all_to_all(out.reshape(chips, own_rows, width), CHIPS, 0, 0, tiled=True)
    return jnp.sum(out.astype(F32), axis=0).astype(BF16)


def solution(mesh):
    side = (4, 8, 2, 8)
    fine = Mesh(mesh.devices.reshape(side), ("x", "y", "c", "z"))
    ad, tp = ("x", "y", "c"), "z"
    placed = (
        P(ad, tp),
        P(ad, tp),
        P(ad, tp),
        P(ad, tp),
        P(ad, tp, None),
        P(ad, tp, None),
        P(None, tp, ad),
        P(None, tp, ad),
        P(ad, None, tp),
        P(ad, None, tp),
        P(),
        P(),
    )
    return jax.shard_map(
        per_device, mesh=fine, in_specs=placed, out_specs=P(ad, tp), check_vma=False
    )
```

```python
import jax
import jax.numpy as jnp
from jax import lax
from jax.sharding import Mesh, PartitionSpec as P

OCAP = 24
LANES = 128
F32 = jnp.float32
BF16 = jnp.bfloat16
NT = (((1,), (1,)), ((), ()))
TN = (((0,), (0,)), ((), ()))
OWN = ("x", "y", "c")
CHIPS = ("x", "y")


def spread(block, axes, count):
    copies = jnp.broadcast_to(block[None], (count,) + block.shape)
    return lax.all_to_all(copies, axes, 0, 0, tiled=True)


def per_device(
    inputs, w_gate, w_up, w_down, a_gate, a_up, b_gate, b_up, a_down, b_down, adapter_ids, owner_map
):
    chips = lax.axis_size("x") * lax.axis_size("y")
    cores = lax.axis_size("c")
    parts = lax.axis_size("z")
    owners = chips * cores
    here_owner = lax.axis_index(OWN)
    own_rows, width = inputs.shape
    rows = adapter_ids.shape[0]
    units = w_gate.shape[0]
    rank = a_gate.shape[2]
    rank_part = b_gate.shape[1]
    slots = owner_map.shape[0]

    swap = [(0, 1), (1, 0)]
    half = jnp.broadcast_to(inputs[None], (chips,) + inputs.shape)
    half, a_gate, a_up, b_down = lax.optimization_barrier((half, a_gate, a_up, b_down))
    half = lax.all_to_all(half, CHIPS, 0, 0, tiled=True)
    factors = jnp.concatenate([a_gate[0].T, a_up[0].T, b_down[0]], axis=0)
    other = lax.ppermute(factors, "c", swap)
    shrink_pair = (factors[: 2 * rank], other[: 2 * rank])
    down_pair = jnp.concatenate([factors[2 * rank :], other[2 * rank :]], axis=0)
    half = half.reshape(chips * own_rows, width)

    adapter = adapter_ids[:, 0]
    table = jnp.arange(slots, dtype=jnp.int32)
    row_slot = jnp.sum(jnp.where(adapter[:, None] == table[None, :], owner_map[None, :], 0), axis=1)
    onehot = (row_slot[:, None] == table[None, :]).astype(jnp.int32)
    position = jnp.sum((jnp.cumsum(onehot, axis=0) - onehot) * onehot, axis=1)

    def ordered(values):
        by_core = values.reshape(chips, cores, own_rows).transpose(1, 0, 2)
        by_core = by_core.reshape(cores, chips * own_rows)
        return jnp.where(lax.axis_index("c") == 0, by_core, by_core[::-1]).reshape(rows)

    row_slot, position = ordered(row_slot), ordered(position)
    half_rows = chips * own_rows
    here_core = lax.axis_index("c")
    row_core = jnp.where(jnp.arange(rows) < half_rows, here_core, 1 - here_core)
    worker = row_slot - row_slot % cores + row_core
    apart = (row_slot % cores) ^ row_core
    seat = apart * OCAP + position
    seats = cores * OCAP
    seat_of = jnp.arange(seats, dtype=jnp.int32)
    lane = jnp.arange(LANES, dtype=jnp.int32)
    up_per = LANES // (2 * rank_part)
    up_lines = seats // up_per
    mine = (worker == here_owner)[:half_rows, None] & (seat[:half_rows, None] == seat_of[None, :])
    mine = mine.astype(BF16)
    up_line = worker * up_lines + seat // up_per
    up_lines_all = jnp.arange(owners * up_lines, dtype=jnp.int32)
    up_pick = (up_line[:, None] == up_lines_all[None, :]).astype(BF16)
    up_lane = lane[:, None] // (2 * rank_part) == (seat % up_per)[None, :]
    down_per = LANES // rank_part
    down_lines = seats // down_per
    down_line = worker * down_lines + seat // down_per
    down_lines_all = jnp.arange(owners * down_lines, dtype=jnp.int32)
    down_pick = (down_lines_all[:, None] == down_line[None, :]).astype(BF16)
    down_seat = jnp.arange(down_per, dtype=jnp.int32)[:, None] == (seat % down_per)[None, :]
    down_seat = down_seat.astype(BF16)[:, None, :]
    our_line = down_line[:half_rows, None] - here_owner * down_lines
    ours = (our_line == jnp.arange(down_lines, dtype=jnp.int32)[None, :]).astype(BF16)
    our_seat = (seat % down_per)[:half_rows, None] == (lane // rank_part)[None, :]
    our_slot = jnp.arange(cores * rank, dtype=jnp.int32)[None, :] // rank == apart[:half_rows, None]
    slot_rows = (table[:, None] == row_slot[None, :]).astype(BF16)

    column = jnp.arange(parts * LANES, dtype=jnp.int32)
    gathered = column // LANES * rank_part + column % rank_part
    fold = gathered[:, None] == jnp.arange(cores * rank, dtype=jnp.int32)[None, :] % rank
    masks = (
        slot_rows,
        slot_rows.astype(F32),
        down_pick,
        down_seat,
        ours,
        our_seat.astype(BF16),
        our_slot.astype(BF16),
        up_pick,
        fold.astype(BF16),
        shrink_pair,
    )
    half, masks = lax.optimization_barrier((half, masks))
    slot_rows, slot_mask, down_pick, down_seat, ours, our_seat, our_slot, up_pick = masks[:8]
    fold, shrink_pair = masks[8:]
    selected = lax.dot_general(mine, half, TN, preferred_element_type=F32).astype(BF16)
    shrunk = jnp.concatenate(
        [
            lax.dot_general(
                selected[u * OCAP : (u + 1) * OCAP],
                shrink_pair[u],
                NT,
                preferred_element_type=F32,
            )
            for u in range(cores)
        ],
        axis=0,
    ).astype(BF16)
    part, seat_up = column // LANES, column % LANES // (2 * rank_part)
    low = column % (2 * rank_part)
    source = part * rank_part + low % rank_part + low // rank_part * rank
    move = (jnp.arange(2 * rank, dtype=jnp.int32)[:, None] == source[None, :]).astype(BF16)
    shrunk = jnp.dot(shrunk, move, preferred_element_type=F32)
    shrunk = jnp.where(seat_of[:, None] % up_per == seat_up[None, :], shrunk, 0).astype(BF16)
    line_of = jnp.arange(up_lines, dtype=jnp.int32)[:, None] == seat_of[None, :] // up_per
    shrunk = jnp.dot(line_of.astype(BF16), shrunk, preferred_element_type=F32).astype(BF16)
    shrunk = shrunk.reshape(up_lines, parts, LANES).transpose(1, 0, 2)
    shrunk = lax.all_to_all(shrunk, "z", 0, 0, tiled=True)
    half, shrunk = lax.optimization_barrier((half, shrunk))
    piece = jnp.concatenate([half, lax.ppermute(half, "c", swap)], axis=0)
    shrunk = jnp.sum(shrunk.astype(F32), axis=0).astype(BF16)
    low_all = spread(shrunk, OWN, owners)
    gate_base = lax.dot_general(w_gate, piece, NT, preferred_element_type=F32)
    up_base = lax.dot_general(w_up, piece, NT, preferred_element_type=F32)
    low_all, gate_base, up_base = lax.optimization_barrier((low_all, gate_base, up_base))
    low_rows = lax.dot_general(
        low_all.reshape(owners * up_lines, LANES),
        up_pick,
        (((0,), (1,)), ((), ())),
        preferred_element_type=F32,
    )
    low_rows = jnp.where(up_lane, low_rows, 0).astype(BF16)
    gather_up = jnp.arange(2 * rank_part, dtype=jnp.int32)[:, None] == lane[None, :] % (2 * rank_part)
    low_rows = jnp.dot(gather_up.astype(BF16), low_rows, preferred_element_type=F32).astype(BF16)

    def expand(low, weights):
        wide = (slot_rows[:, None, :] * low[None, :, :]).reshape(slots * rank_part, rows)
        return lax.dot_general(
            weights.reshape(slots * rank_part, units), wide, TN, preferred_element_type=F32
        )

    gate_part = gate_base + expand(low_rows[:rank_part], b_gate)
    up_part = up_base + expand(low_rows[rank_part:], b_up)
    both = jnp.stack(
        [
            gate_part.astype(BF16).reshape(parts, units // parts, rows),
            up_part.astype(BF16).reshape(parts, units // parts, rows),
        ],
        axis=1,
    )
    both = lax.all_to_all(both, "z", 0, 0, tiled=True)
    both = jnp.sum(both.astype(F32), axis=0)
    hidden = (jax.nn.silu(both[0]) * both[1]).astype(BF16)
    hidden_all = spread(hidden, "z", parts).reshape(units, rows)

    rank_full = lax.dot_general(
        a_down.reshape(units, slots * rank_part), hidden_all, TN, preferred_element_type=F32
    )
    rank_rows = jnp.sum(
        rank_full.reshape(slots, rank_part, rows) * slot_mask[:, None, :], axis=0
    ).astype(BF16)
    rank_wide = (down_seat * rank_rows[None, :, :]).reshape(LANES, rows)
    rank_sent = lax.dot_general(down_pick, rank_wide, NT, preferred_element_type=F32).astype(BF16)
    rank_sum = lax.all_to_all(
        rank_sent.reshape(owners, down_lines, LANES), OWN, 0, 0, tiled=True
    )
    out = lax.dot_general(hidden_all, w_down, TN, preferred_element_type=F32)
    kept, given = out[:half_rows], out[half_rows:].astype(BF16)
    rank_sum, kept, given = lax.optimization_barrier((rank_sum, kept, given))
    rank_sum = jnp.sum(rank_sum.astype(F32), axis=0).astype(BF16)
    rank_all = spread(rank_sum, "z", parts)
    out = kept + lax.ppermute(given, "c", swap).astype(F32)
    rank_ours = lax.dot_general(
        ours, rank_all, (((1,), (1,)), ((), ())), preferred_element_type=F32
    )
    rank_ours = rank_ours.astype(BF16) * our_seat[:, None, :]
    rank_ours = jnp.dot(
        rank_ours.reshape(half_rows, parts * LANES),
        fold,
        preferred_element_type=F32,
    )
    rank_ours = rank_ours.astype(BF16) * our_slot
    out = out + jnp.dot(rank_ours, down_pair, preferred_element_type=F32)
    out = out.astype(BF16)
    out = lax.all_to_all(out.reshape(chips, own_rows, width), CHIPS, 0, 0, tiled=True)
    return jnp.sum(out.astype(F32), axis=0).astype(BF16)


def solution(mesh):
    side = (4, 8, 2, 8)
    fine = Mesh(mesh.devices.reshape(side), ("x", "y", "c", "z"))
    ad, tp = ("x", "y", "c"), "z"
    placed = (
        P(ad, tp),
        P(ad, tp),
        P(ad, tp),
        P(ad, tp),
        P(ad, tp, None),
        P(ad, tp, None),
        P(None, tp, ad),
        P(None, tp, ad),
        P(ad, None, tp),
        P(ad, None, tp),
        P(),
        P(),
    )
    return jax.shard_map(
        per_device, mesh=fine, in_specs=placed, out_specs=P(ad, tp), check_vma=False
    )
```
